32 devices in a mesh: rhs: 16 (over z, x, core), fac: 2 (over y).
Axes of the slice: x: 2, y: 2, z: 4, core: 2. Of those that a mesh axis runs over, the one named last changes fastest.
Arguments:
- right_sides: bfloat16 [1024, 768], P('rhs', 'fac'), may hold values from -6 to 6
- stripe: bfloat16 [768, 768], P('fac', 'rhs'), may hold values from -0.109375 to 0.109375
- inverses: float32 [2, 384, 384], P('fac'), may hold values from -2 to 2, as said below
- structure: int32 [2, 2], replicated, may hold values 0 or 1
- heater_wattages: bfloat16 [256, 1024], P(None, 'rhs'), may hold values from -0.25 to 0.25
Outputs:
- unknown_vector_results: bfloat16 [1024, 768], P('rhs', 'fac')
- thermal_field_reply: float32 [256, 768], P('rhs', 'fac')
The draws below stay inside these ranges and needn't reach their ends.
Inputs may be any that keep to these rules, and one draw needn't show every extreme that they name: Each inverses[s] is lower triangular with its diagonal between 0.5 and 2.
All inputs are finite; a program needn't handle non-finite values.
Results may differ from the reference program's by a relative error of at most 0.0095.
Values may be sent and summed in bfloat16 or wider, within the bound.
A program may use at most 64 MiB of HBM per device.

```python
import jax
import jax.numpy as jnp
from jax import lax

W = 384
K = 256
NS = 2
N = 768
NRHS = 1024


def draw_inverses(key, part):
    first, second = jax.random.split(jax.random.fold_in(key, 17))
    diagonal = jnp.exp(jax.random.uniform(first, (NS, W), jnp.float32, jnp.log(0.5), jnp.log(2.0)))
    lower = jax.random.normal(second, (NS, W, W), jnp.float32) * (0.6 / jnp.sqrt(1.0 * W))
    below = jnp.tril(jnp.ones((W, W), jnp.float32), -1)
    return lower * below + jnp.eye(W, dtype=jnp.float32) * diagonal[:, :, None]


def plant(values, own_key, least, high):
    longest = values.shape.index(max(values.shape))
    spots = []
    for shift in (0, 1):
        where = [jax.random.randint(jax.random.fold_in(own_key, axis), (), 0, length) for axis, length in enumerate(values.shape)]
        where[longest] = (where[longest] + shift) % values.shape[longest]
        spots.append(tuple(where))
    return values.at[spots[0]].set(least).at[spots[1]].set(high)


def raised(result, stream_key, source, target, blocks, factor):
    owner, partner = [(jnp.arange(result.shape[dim]) // (result.shape[dim] // blocks)).reshape([-1 if axis == dim else 1 for axis in range(result.ndim)]) for dim in (source, target)]
    chosen = jax.random.permutation(stream_key, blocks)[partner]
    strong = (owner == chosen) | (owner == (partner + blocks // 2) % blocks)
    return jnp.where(strong, factor * result, result)


def block_scale(own_key, dims, cuts, least, top_value):
    gain = 1.0
    for position, shards_of in cuts:
        draws = jax.random.uniform(jax.random.fold_in(jax.random.fold_in(own_key, 6), position), (shards_of,), jnp.float32, least / len(cuts), top_value / len(cuts))
        gain = gain * jnp.repeat(jnp.exp(draws), dims[position] // shards_of).reshape((-1,) + (1,) * (len(dims) - 1 - position))
    return gain


def bell_draw(rng, dims, width, limit, shards=(), held_as=jnp.bfloat16):
    loudness = block_scale(rng, dims, shards, -0.22, 0.18) if shards else 1.0
    values = jax.random.normal(rng, dims, jnp.float32) * width * loudness
    return jnp.minimum(jnp.maximum(values, -limit), limit).astype(held_as)


def noise_with(rng, dims, deviation, limit, cuts, heavy, held_as=jnp.bfloat16):
    drawn = deviation * jax.random.normal(rng, dims, jnp.float32)
    if cuts:
        drawn = drawn * block_scale(rng, dims, cuts, -0.22, 0.18)
    return jnp.clip(raised(drawn, jax.random.fold_in(rng, 3), *heavy), -limit, limit).astype(held_as)


def setup_inputs(seed: int = 0) -> dict:
    seeds = jax.random.split(jax.random.key(seed), 6)
    right_sides = bell_draw(seeds[0], (NRHS, N), 1.0, 6.0, ((0, 16), (1, 2)))
    stripe = bell_draw(seeds[1], (N, N), (4 * N) ** -0.5, 0.109375, ((0, 2), (1, 16)))
    inverses = draw_inverses(jax.random.fold_in(seeds[5], 71), 0)
    structure = plant((jax.random.randint(seeds[3], (NS, NS), 0, 4) < 3).astype(jnp.int32), jax.random.fold_in(seeds[3], 1), 0, 1)
    heater_wattages = noise_with(seeds[4], (K, NRHS), NRHS ** -0.5, 0.25, ((1, 16),), (1, 0, 16, 2.0))
    return {"right_sides": right_sides, "stripe": stripe, "inverses": inverses, "structure": structure, "heater_wattages": heater_wattages}


def against_rows(left, right):
    return lax.dot_general(left, right, (((1,), (1,)), ((), ())), preferred_element_type=jnp.float32)


def reference(right_sides, stripe, inverses, structure, heater_wattages):
    total_rows = NS * W
    forward_sweep = jnp.zeros((NRHS, total_rows), jnp.bfloat16)
    for block in range(NS):
        col_mask = jnp.repeat(structure[block], W).astype(jnp.bfloat16)
        update = against_rows(forward_sweep * col_mask, stripe[block * W:(block + 1) * W])
        remainder = right_sides[:, block * W:(block + 1) * W].astype(jnp.float32) - update
        finished_unknowns = jnp.dot(remainder, inverses[block].T, precision=lax.Precision.HIGHEST)
        forward_sweep = forward_sweep.at[:, block * W:(block + 1) * W].set(finished_unknowns.astype(jnp.bfloat16))
    unknown_vector_results = jnp.zeros((NRHS, total_rows), jnp.bfloat16)
    for block in range(NS - 1, -1, -1):
        row_mask = jnp.repeat(structure[:, block], W).astype(jnp.bfloat16)
        update = jnp.dot(unknown_vector_results * row_mask, stripe[:, block * W:(block + 1) * W], preferred_element_type=jnp.float32)
        remainder = forward_sweep[:, block * W:(block + 1) * W].astype(jnp.float32) - update
        finished_unknowns = jnp.dot(remainder, inverses[block], precision=lax.Precision.HIGHEST)
        unknown_vector_results = unknown_vector_results.at[:, block * W:(block + 1) * W].set(finished_unknowns.astype(jnp.bfloat16))
    thermal_field_reply = jnp.dot(heater_wattages, unknown_vector_results, preferred_element_type=jnp.float32)
    return unknown_vector_results, thermal_field_reply
```

```python
import functools

import jax
import jax.numpy as jnp
from jax import lax
from jax.experimental import pallas as pl
from jax.experimental.pallas import tpu as pltpu
from jax.sharding import PartitionSpec as P

F32 = jnp.float32
BF16 = jnp.bfloat16
NT = (((1,), (1,)), ((), ()))
NN = (((1,), (0,)), ((), ()))


def mul(left, right, dims):
    return lax.dot_general(left, right, dims, preferred_element_type=F32)


def split(value):
    high = value.astype(BF16)
    return high, (value - high.astype(F32)).astype(BF16)


def kernel(
    shape, sides_ref, stripe_ref, inverse_ref, structure_ref, watts_ref, out_ref, reply_ref,
    factor, high, low, acc, fwd, fwd_in, upd_out, upd_in, part, pair_out, pair_in, mine,
    sum_out, sum_in, z_send, x_send, c_send, factor_recv, f_send, f_recv, u_send, u_recv,
    pair_send, pair_recv, s_send, s_recv,
):
    supers, ranks, zs, xs = shape
    groups = ranks // 2
    width = inverse_ref.shape[1]
    count = sides_ref.shape[0]
    per = width // factor.shape[1]
    s = lax.axis_index("fac")
    me = lax.axis_index("rhs")
    core = lax.rem(me, 2)
    chip = lax.div(me, 2)
    x = lax.rem(chip, xs)
    z = lax.div(chip, xs)

    def rank(zz, xx, cc):
        return (zz * xs + xx) * 2 + cc

    def needed(b):
        return b < s * per

    barrier = pltpu.get_barrier_semaphore()
    for k in range(1, ranks):
        pl.semaphore_signal(barrier, inc=1, device_id={"rhs": lax.rem(me + k, ranks)})
    for k in range(1, supers):
        pl.semaphore_signal(barrier, inc=1, device_id={"fac": lax.rem(s + k, supers)})

    columns = factor.shape[1]

    @pl.when(needed(me))
    def _():
        eye = (
            lax.broadcasted_iota(jnp.int32, (columns, columns), 0)
            == lax.broadcasted_iota(jnp.int32, (columns, columns), 1)
        ).astype(F32).astype(BF16)
        factor[me] = mul(eye, stripe_ref[...], NT).astype(BF16)

    h, l = split(inverse_ref[0])
    high[...] = h
    low[...] = l
    acc[...] = sides_ref[...].astype(F32)

    def times_inverse(dims):
        a_high, a_low = split(acc[...])
        both = mul(jnp.concatenate([a_high, a_low], axis=0), high[...], dims)
        return both[:count] + both[count:] + mul(a_high, low[...], dims)

    @pl.when(s == 0)
    def _():
        fwd[...] = times_inverse(NT).astype(BF16)

    pl.semaphore_wait(barrier, ranks - 1 + supers - 1)

    def factor_copy(b, send, where):
        return pltpu.make_async_remote_copy(
            src_ref=factor.at[b], dst_ref=factor.at[b], send_sem=send,
            recv_sem=factor_recv.at[b], device_id={"rhs": where},
        )

    def forward_copy(t, k, where):
        return pltpu.make_async_remote_copy(
            src_ref=fwd, dst_ref=fwd_in.at[t], send_sem=f_send.at[k],
            recv_sem=f_recv.at[t], device_id={"fac": where},
        )

    def update_copy(t, where):
        return pltpu.make_async_remote_copy(
            src_ref=upd_out.at[where], dst_ref=upd_in.at[t], send_sem=u_send.at[where],
            recv_sem=u_recv.at[t], device_id={"fac": where},
        )

    @pl.when(s == 0)
    def _():
        for k in range(1, supers):
            forward_copy(0, k, k).start()

    for k in range(1, zs):
        @pl.when(needed(me))
        def _():
            factor_copy(me, z_send.at[k], rank(lax.rem(z + k, zs), x, core)).start()
    for k in range(zs):
        zz = lax.rem(z + zs - k, zs)
        b = rank(zz, x, core)

        @pl.when(needed(b))
        def _():
            if k > 0:
                factor_copy(b, z_send.at[0], me).wait_recv()
            for j in range(1, xs):
                factor_copy(b, x_send.at[k, j], rank(z, lax.rem(x + j, xs), core)).start()
            factor_copy(b, c_send.at[k, 0], rank(z, x, 1 - core)).start()
    for k in range(zs):
        zz = lax.rem(z + zs - k, zs)
        for j in range(1, xs):
            b = rank(zz, lax.rem(x + xs - j, xs), core)

            @pl.when(needed(b))
            def _():
                factor_copy(b, z_send.at[0], me).wait_recv()
                factor_copy(b, c_send.at[k, j], rank(z, x, 1 - core)).start()
    for zz in range(zs):
        for xx in range(xs):
            b = rank(zz, xx, 1 - core)

            @pl.when(needed(b))
            def _():
                factor_copy(b, z_send.at[0], me).wait_recv()

    def block(t):
        return factor[t * per:(t + 1) * per].reshape(width, width)

    for t in range(supers - 1):
        @pl.when(s > t)
        def _():
            forward_copy(t, 0, s).wait_recv()
            keep = structure_ref[s, t].astype(F32)
            acc[...] -= keep * mul(fwd_in[t], block(t), NN)

    @pl.when(s > 0)
    def _():
        fwd[...] = times_inverse(NT).astype(BF16)

    for k in range(2, supers):
        @pl.when((s > 0) & (s < k))
        def _():
            forward_copy(s, k, k).start()

    acc[...] = fwd[...].astype(F32)
    for t in range(supers - 1, 0, -1):
        @pl.when(s < t)
        def _():
            update_copy(t, s).wait_recv()
            acc[...] -= upd_in[t].astype(F32)
    solved = times_inverse(NN).astype(BF16)
    out_ref[...] = solved
    for t in range(supers - 2, -1, -1):
        @pl.when(s > t)
        def _():
            keep = structure_ref[s, t].astype(F32)
            upd_out[t] = (keep * mul(out_ref[...], block(t), NT)).astype(BF16)
            update_copy(s, t).start()

    part[...] = mul(watts_ref[...], out_ref[...], NN).reshape(part.shape)
    for g in range(groups):
        pair_out[g] = part[2 * g + 1 - core].astype(pair_out.dtype)
    pair = pltpu.make_async_remote_copy(
        src_ref=pair_out, dst_ref=pair_in, send_sem=pair_send, recv_sem=pair_recv,
        device_id={"rhs": rank(z, x, 1 - core)},
    )
    pair.start()
    pair.wait_recv()
    for g in range(groups):
        both = part[2 * g + core] + pair_in[g].astype(F32)
        mine[g] = both
        sum_out[g] = both.astype(sum_out.dtype)

    def sum_copy(target, source, k):
        return pltpu.make_async_remote_copy(
            src_ref=sum_out.at[target], dst_ref=sum_in.at[source], send_sem=s_send.at[k],
            recv_sem=s_recv.at[source], device_id={"rhs": target * 2 + core},
        )

    for k in range(1, groups):
        sum_copy(lax.rem(chip + k, groups), chip, k).start()
    total = mine[chip]
    for k in range(1, groups):
        source = lax.rem(chip + groups - k, groups)
        sum_copy(chip, source, 0).wait_recv()
        total = total + sum_in[source].astype(F32)
    reply_ref[...] = total

    for k in range(1, groups):
        sum_copy(lax.rem(chip + k, groups), chip, k).wait_send()
    pair.wait_send()
    for t in range(supers - 1):
        @pl.when(s > t)
        def _():
            update_copy(s, t).wait_send()
    for k in range(1, supers):
        @pl.when(s < k)
        def _():
            forward_copy(s, k, k).wait_send()
    for k in range(1, zs):
        @pl.when(needed(me))
        def _():
            factor_copy(me, z_send.at[k], me).wait_send()
    for k in range(zs):
        zz = lax.rem(z + zs - k, zs)
        for j in range(xs):
            b = rank(zz, lax.rem(x + xs - j, xs), core)

            @pl.when(needed(b))
            def _():
                factor_copy(b, c_send.at[k, j], me).wait_send()
            if j > 0:
                own = rank(zz, x, core)

                @pl.when(needed(own))
                def _():
                    factor_copy(own, x_send.at[k, j], me).wait_send()


def body(right_sides, stripe, inverses, structure, heater_wattages):
    supers = lax.axis_size("fac")
    ranks = lax.axis_size("rhs")
    zs = 4
    xs = ranks // (2 * zs)
    count, width = right_sides.shape
    columns = stripe.shape[1]
    loads = heater_wattages.shape[0]
    rows = loads // ranks
    groups = ranks // 2
    wire = BF16 if rows % 16 == 0 else F32
    dma = pltpu.SemaphoreType.DMA
    vmem = pl.BlockSpec(memory_space=pltpu.VMEM)
    return pl.pallas_call(
        functools.partial(kernel, (supers, ranks, zs, xs)),
        out_shape=(
            jax.ShapeDtypeStruct((count, width), BF16),
            jax.ShapeDtypeStruct((rows, width), F32),
        ),
        in_specs=[vmem, vmem, vmem, pl.BlockSpec(memory_space=pltpu.SMEM), vmem],
        out_specs=(vmem, vmem),
        scratch_shapes=[
            pltpu.VMEM((ranks, columns, width), BF16),
            pltpu.VMEM((width, width), BF16),
            pltpu.VMEM((width, width), BF16),
            pltpu.VMEM((count, width), F32),
            pltpu.VMEM((count, width), BF16),
            pltpu.VMEM((supers, count, width), BF16),
            pltpu.VMEM((supers, count, width), BF16),
            pltpu.VMEM((supers, count, width), BF16),
            pltpu.VMEM((ranks, rows, width), F32),
            pltpu.VMEM((groups, rows, width), wire),
            pltpu.VMEM((groups, rows, width), wire),
            pltpu.VMEM((groups, rows, width), F32),
            pltpu.VMEM((groups, rows, width), wire),
            pltpu.VMEM((groups, rows, width), wire),
            dma((zs,)), dma((zs, xs)), dma((zs, xs)), dma((ranks,)),
            dma((supers,)), dma((supers,)), dma((supers,)), dma((supers,)),
            dma, dma, dma((groups,)), dma((groups,)),
        ],
        compiler_params=pltpu.CompilerParams(
            collective_id=0, has_side_effects=True, vmem_limit_bytes=32 * 1024 * 1024
        ),
    )(right_sides, stripe, inverses, structure, heater_wattages)


def solution(mesh):
    placed = (P("rhs", "fac"), P("fac", "rhs"), P("fac", None, None), P(), P(None, "rhs"))
    return jax.shard_map(
        body,
        mesh=mesh,
        in_specs=placed,
        out_specs=(P("rhs", "fac"), P("rhs", "fac")),
        check_vma=False,
    )
```

```python
import functools

import jax
import jax.numpy as jnp
from jax import lax
from jax.experimental import pallas as pl
from jax.experimental.pallas import tpu as pltpu
from jax.sharding import PartitionSpec as P

F32 = jnp.float32
BF16 = jnp.bfloat16
LIMIT = 64 * 1024 * 1024 - 160 * 1024
NT = (((1,), (1,)), ((), ()))
NN = (((1,), (0,)), ((), ()))


def mul(left, right, dims):
    return lax.dot_general(left, right, dims, preferred_element_type=F32)


def split(value):
    high = value.astype(BF16)
    return high, (value - high.astype(F32)).astype(BF16)


def kernel(
    shape, sides_any, stripe_any, inverse_any, structure_any, watts_any, out_any, reply_ref,
    out_ref, factor, sides, inverse, keeps, watts_in, watts, watts_own, plain, turned, base, fwd, fwd_in,
    upd_out, upd_in, pair_out, pair_in, mine, sum_out, sum_in,
    load, z_send, x_send, c_send, factor_recv, f_send, f_recv, u_send, u_recv,
    pair_send, pair_recv, s_send, s_recv,
):
    supers, ranks, zs, xs = shape
    groups = ranks // 2
    width = inverse.shape[0]
    per = width // factor.shape[1]
    s = lax.axis_index("fac")
    me = lax.axis_index("rhs")
    core = lax.rem(me, 2)
    chip = lax.div(me, 2)
    x = lax.rem(chip, xs)
    z = lax.div(chip, xs)

    def rank(zz, xx, cc):
        return (zz * xs + xx) * 2 + cc

    def needed(b):
        return b < s * per

    loads = [
        pltpu.make_async_copy(stripe_any, factor.at[me], load.at[0]),
        pltpu.make_async_copy(inverse_any.at[0], inverse, load.at[1]),
        pltpu.make_async_copy(sides_any, sides, load.at[2]),
        pltpu.make_async_copy(watts_any, watts_in, load.at[3]),
        pltpu.make_async_copy(structure_any, keeps, load.at[4]),
    ]
    for copy in loads:
        copy.start()

    barrier = pltpu.get_barrier_semaphore()
    pl.semaphore_signal(barrier, inc=1, device_id={"rhs": chip * 2 + 1 - core})
    for k in range(1, supers):
        pl.semaphore_signal(barrier, inc=1, device_id={"fac": lax.rem(s + k, supers)})
    for k in range(1, groups):
        pl.semaphore_signal(barrier, inc=1, device_id={"rhs": lax.rem(chip + k, groups) * 2 + core})
    loads[0].wait()
    pl.semaphore_wait(barrier, groups + supers - 1)

    def factor_copy(b, send, where):
        return pltpu.make_async_remote_copy(
            src_ref=factor.at[b], dst_ref=factor.at[b], send_sem=send,
            recv_sem=factor_recv.at[b], device_id={"rhs": where},
        )

    def forward_copy(t, k, where):
        return pltpu.make_async_remote_copy(
            src_ref=fwd, dst_ref=fwd_in.at[t], send_sem=f_send.at[k],
            recv_sem=f_recv.at[t], device_id={"fac": where},
        )

    def update_copy(t, where):
        return pltpu.make_async_remote_copy(
            src_ref=upd_out.at[where], dst_ref=upd_in.at[t], send_sem=u_send.at[where],
            recv_sem=u_recv.at[t], device_id={"fac": where},
        )

    @pl.when(needed(me))
    def _():
        for k in range(1, zs):
            factor_copy(me, z_send.at[k], rank(lax.rem(z + k, zs), x, core)).start()

    def relay(k):
        b = rank(lax.rem(z + zs - k, zs), x, core)

        @pl.when(needed(b))
        def _():
            if k > 0:
                factor_copy(b, z_send.at[0], me).wait_recv()
            for j in range(1, xs):
                factor_copy(b, x_send.at[k, j], rank(z, lax.rem(x + j, xs), core)).start()
            factor_copy(b, c_send.at[k, 0], rank(z, x, 1 - core)).start()

    relay(0)

    loads[1].wait()
    high, low = split(inverse[...])
    plain[:width] = high
    plain[width:] = low
    turned[:, :width] = high
    turned[:, width:2 * width] = low
    turned[:, 2 * width:] = high
    loads[2].wait()
    loads[4].wait()

    def twice(value):
        return jnp.concatenate([value, value], axis=1)

    def thrice(value):
        a_high, a_low = split(value)
        return jnp.concatenate([a_high, a_high, a_low], axis=1)

    @pl.when(s == 0)
    def _():
        fwd[...] = mul(twice(sides[...]), turned[:, :2 * width], NT).astype(BF16)
        for k in range(1, supers):
            forward_copy(0, k, k).start()

    for k in range(1, zs):
        relay(k)
    for k in range(zs):
        for j in range(1, xs):
            b = rank(lax.rem(z + zs - k, zs), lax.rem(x + xs - j, xs), core)

            @pl.when(needed(b))
            def _():
                factor_copy(b, z_send.at[0], me).wait_recv()
                factor_copy(b, c_send.at[k, j], rank(z, x, 1 - core)).start()

    loads[3].wait()
    watts[...] = watts_in[...].astype(F32).T.reshape(watts.shape)
    for g in range(groups):
        watts_own[g] = watts[2 * g + 1 - core]
        watts_own[groups + g] = watts[2 * g + core]

    for zz in range(zs):
        for xx in range(xs):
            b = rank(zz, xx, 1 - core)

            @pl.when(needed(b))
            def _():
                factor_copy(b, z_send.at[0], me).wait_recv()

    def block(t):
        return factor[t * per:(t + 1) * per].reshape(width, width)

    @pl.when(s > 0)
    def _():
        base[...] = sides[...].astype(F32)
        for t in range(supers - 1):
            @pl.when(s > t)
            def _():
                forward_copy(t, 0, s).wait_recv()
                keep = keeps[s, t].astype(F32)
                base[...] -= keep * mul(fwd_in[t], block(t), NN)
        fwd[...] = mul(thrice(base[...]), turned[...], NT).astype(BF16)
        for k in range(2, supers):
            @pl.when(s < k)
            def _():
                forward_copy(s, k, k).start()

    base[...] = mul(twice(fwd[...]), plain[...], NN)
    out_ref[...] = base[...].astype(BF16)
    for t in range(supers - 1, 0, -1):
        @pl.when(s < t)
        def _():
            update_copy(t, s).wait_recv()
            base[...] -= mul(twice(upd_in[t]), plain[...], NN)
            if t - 1 == 0:
                out_ref[...] = base[...].astype(BF16)
            else:
                @pl.when(s == t - 1)
                def _():
                    out_ref[...] = base[...].astype(BF16)
    for t in range(supers - 2, -1, -1):
        @pl.when(s > t)
        def _():
            keep = keeps[s, t].astype(F32)
            upd_out[t] = (keep * mul(out_ref[...], block(t), NT)).astype(BF16)
            update_copy(s, t).start()

    def product(first):
        rows = watts_own[first:first + groups]
        rows = rows.reshape(groups * rows.shape[1], rows.shape[2]).astype(BF16)
        return mul(rows, out_ref[...], NN).reshape(mine.shape)

    pair_out[...] = product(0).astype(pair_out.dtype)
    pair = pltpu.make_async_remote_copy(
        src_ref=pair_out, dst_ref=pair_in, send_sem=pair_send, recv_sem=pair_recv,
        device_id={"rhs": rank(z, x, 1 - core)},
    )
    pair.start()
    keep_out = pltpu.make_async_copy(out_ref, out_any, load.at[5])
    keep_out.start()
    mine[...] = product(groups)
    pair.wait_recv()
    both = mine[...] + pair_in[...].astype(F32)
    mine[...] = both
    sum_out[...] = both.astype(sum_out.dtype)

    def sum_copy(target, source, k):
        return pltpu.make_async_remote_copy(
            src_ref=sum_out.at[target], dst_ref=sum_in.at[source], send_sem=s_send.at[k],
            recv_sem=s_recv.at[source], device_id={"rhs": target * 2 + core},
        )

    for k in range(1, groups):
        sum_copy(lax.rem(chip + k, groups), chip, k).start()
    total = mine[chip]
    for k in range(1, groups):
        source = lax.rem(chip + groups - k, groups)
        sum_copy(chip, source, 0).wait_recv()
        total = total + sum_in[source].astype(F32)
    reply_ref[...] = total

    for k in range(1, groups):
        sum_copy(lax.rem(chip + k, groups), chip, k).wait_send()
    pair.wait_send()
    keep_out.wait()
    for t in range(supers - 1):
        @pl.when(s > t)
        def _():
            update_copy(s, t).wait_send()
    for k in range(1, supers):
        @pl.when(s < k)
        def _():
            forward_copy(s, k, k).wait_send()

    @pl.when(needed(me))
    def _():
        for k in range(1, zs):
            factor_copy(me, z_send.at[k], me).wait_send()
    for k in range(zs):
        own = rank(lax.rem(z + zs - k, zs), x, core)

        @pl.when(needed(own))
        def _():
            factor_copy(own, c_send.at[k, 0], me).wait_send()
            for j in range(1, xs):
                factor_copy(own, x_send.at[k, j], me).wait_send()
        for j in range(1, xs):
            b = rank(lax.rem(z + zs - k, zs), lax.rem(x + xs - j, xs), core)

            @pl.when(needed(b))
            def _():
                factor_copy(b, c_send.at[k, j], me).wait_send()


def write_out(solved_ref, reply_ref, solved_out, reply_out, sem):
    first = pltpu.make_async_copy(solved_ref, solved_out, sem.at[0])
    second = pltpu.make_async_copy(reply_ref, reply_out, sem.at[1])
    first.start()
    second.start()
    first.wait()
    second.wait()


def body(right_sides, stripe, inverses, structure, heater_wattages):
    supers = lax.axis_size("fac")
    ranks = lax.axis_size("rhs")
    zs = 4
    xs = ranks // (2 * zs)
    count, width = right_sides.shape
    columns = stripe.shape[1]
    loads = heater_wattages.shape[0]
    rows = loads // ranks
    groups = ranks // 2
    wire = BF16 if rows % 16 == 0 else F32
    dma = pltpu.SemaphoreType.DMA
    vmem = pl.BlockSpec(memory_space=pltpu.VMEM)
    whole = pl.BlockSpec(memory_space=pl.ANY)
    solved, reply = pl.pallas_call(
        functools.partial(kernel, (supers, ranks, zs, xs)),
        out_shape=(
            jax.ShapeDtypeStruct((count, width), BF16),
            jax.ShapeDtypeStruct((rows, width), F32),
        ),
        in_specs=[whole] * 5,
        out_specs=(whole, vmem),
        scratch_shapes=[
            pltpu.VMEM((count, width), BF16),
            pltpu.VMEM((ranks, columns, width), BF16),
            pltpu.VMEM((count, width), BF16),
            pltpu.VMEM((width, width), F32),
            pltpu.SMEM((supers, supers), jnp.int32),
            pltpu.VMEM((count, loads), BF16),
            pltpu.VMEM((ranks, rows, count), F32),
            pltpu.VMEM((ranks, rows, count), F32),
            pltpu.VMEM((2 * width, width), BF16),
            pltpu.VMEM((width, 3 * width), BF16),
            pltpu.VMEM((count, width), F32),
            pltpu.VMEM((count, width), BF16),
            pltpu.VMEM((supers, count, width), BF16),
            pltpu.VMEM((supers, count, width), BF16),
            pltpu.VMEM((supers, count, width), BF16),
            pltpu.VMEM((groups, rows, width), wire),
            pltpu.VMEM((groups, rows, width), wire),
            pltpu.VMEM((groups, rows, width), F32),
            pltpu.VMEM((groups, rows, width), wire),
            pltpu.VMEM((groups, rows, width), wire),
            dma((6,)), dma((zs,)), dma((zs, xs)), dma((zs, xs)), dma((ranks,)),
            dma((supers,)), dma((supers,)), dma((supers,)), dma((supers,)),
            dma, dma, dma((groups,)), dma((groups,)),
        ],
        compiler_params=pltpu.CompilerParams(
            collective_id=0, has_side_effects=True, vmem_limit_bytes=LIMIT
        ),
    )(right_sides, stripe.T, inverses, structure, heater_wattages.T)
    return pl.pallas_call(
        write_out,
        out_shape=(
            jax.ShapeDtypeStruct((count, width), BF16),
            jax.ShapeDtypeStruct((rows, width), F32),
        ),
        in_specs=[whole, whole],
        out_specs=(whole, whole),
        scratch_shapes=[dma((2,))],
    )(solved, reply)


def solution(mesh):
    placed = (P("rhs", "fac"), P("fac", "rhs"), P("fac", None, None), P(), P(None, "rhs"))
    return jax.shard_map(
        body,
        mesh=mesh,
        in_specs=placed,
        out_specs=(P("rhs", "fac"), P("rhs", "fac")),
        check_vma=False,
    )
```

```python
import functools

import jax
import jax.numpy as jnp
from jax import lax
from jax.experimental import pallas as pl
from jax.experimental.pallas import tpu as pltpu
from jax.sharding import PartitionSpec as P

F32 = jnp.float32
BF16 = jnp.bfloat16
LIMIT = 32 * 1024 * 1024
NT = (((1,), (1,)), ((), ()))
NN = (((1,), (0,)), ((), ()))


def mul(left, right, dims):
    return lax.dot_general(left, right, dims, preferred_element_type=F32)


def split(value):
    high = value.astype(BF16)
    return high, (value - high.astype(F32)).astype(BF16)


def kernel(
    shape, sides_any, stripe_any, inverse_any, structure_any, watts_any, out_ref, reply_ref,
    factor, sides, inverse, keeps, watts_in, watts, watts_own, plain, turned, base, fwd, fwd_in,
    upd_out, upd_in, pair_out, pair_in, mine, sum_out, sum_in,
    load, z_send, x_send, c_send, factor_recv, f_send, f_recv, u_send, u_recv,
    pair_send, pair_recv, s_send, s_recv,
):
    supers, ranks, zs, xs = shape
    groups = ranks // 2
    width = inverse.shape[0]
    per = width // factor.shape[1]
    s = lax.axis_index("fac")
    me = lax.axis_index("rhs")
    core = lax.rem(me, 2)
    chip = lax.div(me, 2)
    x = lax.rem(chip, xs)
    z = lax.div(chip, xs)

    def rank(zz, xx, cc):
        return (zz * xs + xx) * 2 + cc

    def needed(b):
        return b < s * per

    loads = [
        pltpu.make_async_copy(stripe_any, factor.at[me], load.at[0]),
        pltpu.make_async_copy(inverse_any.at[0], inverse, load.at[1]),
        pltpu.make_async_copy(sides_any, sides, load.at[2]),
        pltpu.make_async_copy(watts_any, watts_in, load.at[3]),
        pltpu.make_async_copy(structure_any, keeps, load.at[4]),
    ]
    for copy in loads:
        copy.start()

    barrier = pltpu.get_barrier_semaphore()
    pl.semaphore_signal(barrier, inc=1, device_id={"rhs": chip * 2 + 1 - core})
    for k in range(1, supers):
        pl.semaphore_signal(barrier, inc=1, device_id={"fac": lax.rem(s + k, supers)})
    for k in range(1, groups):
        pl.semaphore_signal(barrier, inc=1, device_id={"rhs": lax.rem(chip + k, groups) * 2 + core})
    loads[0].wait()
    pl.semaphore_wait(barrier, groups + supers - 1)

    def factor_copy(b, send, where):
        return pltpu.make_async_remote_copy(
            src_ref=factor.at[b], dst_ref=factor.at[b], send_sem=send,
            recv_sem=factor_recv.at[b], device_id={"rhs": where},
        )

    def forward_copy(t, k, where):
        return pltpu.make_async_remote_copy(
            src_ref=fwd, dst_ref=fwd_in.at[t], send_sem=f_send.at[k],
            recv_sem=f_recv.at[t], device_id={"fac": where},
        )

    def update_copy(t, where):
        return pltpu.make_async_remote_copy(
            src_ref=upd_out.at[where], dst_ref=upd_in.at[t], send_sem=u_send.at[where],
            recv_sem=u_recv.at[t], device_id={"fac": where},
        )

    @pl.when(needed(me))
    def _():
        for k in range(1, zs):
            factor_copy(me, z_send.at[k], rank(lax.rem(z + k, zs), x, core)).start()

    def relay(k):
        b = rank(lax.rem(z + zs - k, zs), x, core)

        @pl.when(needed(b))
        def _():
            if k > 0:
                factor_copy(b, z_send.at[0], me).wait_recv()
            for j in range(1, xs):
                factor_copy(b, x_send.at[k, j], rank(z, lax.rem(x + j, xs), core)).start()
            factor_copy(b, c_send.at[k, 0], rank(z, x, 1 - core)).start()

    relay(0)

    loads[1].wait()
    high, low = split(inverse[...])
    plain[:width] = high
    plain[width:] = low
    turned[:, :width] = high
    turned[:, width:2 * width] = low
    turned[:, 2 * width:] = high
    loads[2].wait()
    loads[4].wait()

    def twice(value):
        return jnp.concatenate([value, value], axis=1)

    def thrice(value):
        a_high, a_low = split(value)
        return jnp.concatenate([a_high, a_high, a_low], axis=1)

    @pl.when(s == 0)
    def _():
        fwd[...] = mul(twice(sides[...]), turned[:, :2 * width], NT).astype(BF16)
        for k in range(1, supers):
            forward_copy(0, k, k).start()

    for k in range(1, zs):
        relay(k)
    for k in range(zs):
        for j in range(1, xs):
            b = rank(lax.rem(z + zs - k, zs), lax.rem(x + xs - j, xs), core)

            @pl.when(needed(b))
            def _():
                factor_copy(b, z_send.at[0], me).wait_recv()
                factor_copy(b, c_send.at[k, j], rank(z, x, 1 - core)).start()

    loads[3].wait()
    watts[...] = watts_in[...].astype(F32).T.reshape(watts.shape)
    for g in range(groups):
        watts_own[g] = watts[2 * g + 1 - core]
        watts_own[groups + g] = watts[2 * g + core]

    for zz in range(zs):
        for xx in range(xs):
            b = rank(zz, xx, 1 - core)

            @pl.when(needed(b))
            def _():
                factor_copy(b, z_send.at[0], me).wait_recv()

    def block(t):
        return factor[t * per:(t + 1) * per].reshape(width, width)

    @pl.when(s > 0)
    def _():
        base[...] = sides[...].astype(F32)
        for t in range(supers - 1):
            @pl.when(s > t)
            def _():
                forward_copy(t, 0, s).wait_recv()
                keep = keeps[s, t].astype(F32)
                base[...] -= keep * mul(fwd_in[t], block(t), NN)
        fwd[...] = mul(thrice(base[...]), turned[...], NT).astype(BF16)
        for k in range(2, supers):
            @pl.when(s < k)
            def _():
                forward_copy(s, k, k).start()

    base[...] = mul(twice(fwd[...]), plain[...], NN)
    out_ref[...] = base[...].astype(BF16)
    for t in range(supers - 1, 0, -1):
        @pl.when(s < t)
        def _():
            update_copy(t, s).wait_recv()
            base[...] -= mul(twice(upd_in[t]), plain[...], NN)
            if t - 1 == 0:
                out_ref[...] = base[...].astype(BF16)
            else:
                @pl.when(s == t - 1)
                def _():
                    out_ref[...] = base[...].astype(BF16)
    for t in range(supers - 2, -1, -1):
        @pl.when(s > t)
        def _():
            keep = keeps[s, t].astype(F32)
            upd_out[t] = (keep * mul(out_ref[...], block(t), NT)).astype(BF16)
            update_copy(s, t).start()

    def product(first):
        rows = watts_own[first:first + groups]
        rows = rows.reshape(groups * rows.shape[1], rows.shape[2]).astype(BF16)
        return mul(rows, out_ref[...], NN).reshape(mine.shape)

    pair_out[...] = product(0).astype(pair_out.dtype)
    pair = pltpu.make_async_remote_copy(
        src_ref=pair_out, dst_ref=pair_in, send_sem=pair_send, recv_sem=pair_recv,
        device_id={"rhs": rank(z, x, 1 - core)},
    )
    pair.start()
    mine[...] = product(groups)
    pair.wait_recv()
    both = mine[...] + pair_in[...].astype(F32)
    mine[...] = both
    sum_out[...] = both.astype(sum_out.dtype)

    def sum_copy(target, source, k):
        return pltpu.make_async_remote_copy(
            src_ref=sum_out.at[target], dst_ref=sum_in.at[source], send_sem=s_send.at[k],
            recv_sem=s_recv.at[source], device_id={"rhs": target * 2 + core},
        )

    for k in range(1, groups):
        sum_copy(lax.rem(chip + k, groups), chip, k).start()
    total = mine[chip]
    for k in range(1, groups):
        source = lax.rem(chip + groups - k, groups)
        sum_copy(chip, source, 0).wait_recv()
        total = total + sum_in[source].astype(F32)
    reply_ref[...] = total

    for k in range(1, groups):
        sum_copy(lax.rem(chip + k, groups), chip, k).wait_send()
    pair.wait_send()
    for t in range(supers - 1):
        @pl.when(s > t)
        def _():
            update_copy(s, t).wait_send()
    for k in range(1, supers):
        @pl.when(s < k)
        def _():
            forward_copy(s, k, k).wait_send()

    @pl.when(needed(me))
    def _():
        for k in range(1, zs):
            factor_copy(me, z_send.at[k], me).wait_send()
    for k in range(zs):
        own = rank(lax.rem(z + zs - k, zs), x, core)

        @pl.when(needed(own))
        def _():
            factor_copy(own, c_send.at[k, 0], me).wait_send()
            for j in range(1, xs):
                factor_copy(own, x_send.at[k, j], me).wait_send()
        for j in range(1, xs):
            b = rank(lax.rem(z + zs - k, zs), lax.rem(x + xs - j, xs), core)

            @pl.when(needed(b))
            def _():
                factor_copy(b, c_send.at[k, j], me).wait_send()


def write_out(solved_ref, reply_ref, solved_out, reply_out, sem):
    first = pltpu.make_async_copy(solved_ref, solved_out, sem.at[0])
    second = pltpu.make_async_copy(reply_ref, reply_out, sem.at[1])
    first.start()
    second.start()
    first.wait()
    second.wait()


def body(right_sides, stripe, inverses, structure, heater_wattages):
    supers = lax.axis_size("fac")
    ranks = lax.axis_size("rhs")
    zs = 4
    xs = ranks // (2 * zs)
    count, width = right_sides.shape
    columns = stripe.shape[1]
    loads = heater_wattages.shape[0]
    rows = loads // ranks
    groups = ranks // 2
    wire = BF16 if rows % 16 == 0 else F32
    dma = pltpu.SemaphoreType.DMA
    vmem = pl.BlockSpec(memory_space=pltpu.VMEM)
    whole = pl.BlockSpec(memory_space=pl.ANY)
    solved, reply = pl.pallas_call(
        functools.partial(kernel, (supers, ranks, zs, xs)),
        out_shape=(
            pltpu.VMEM((count, width), BF16),
            pltpu.VMEM((rows, width), F32),
        ),
        in_specs=[whole] * 5,
        out_specs=(vmem, vmem),
        scratch_shapes=[
            pltpu.VMEM((ranks, columns, width), BF16),
            pltpu.VMEM((count, width), BF16),
            pltpu.VMEM((width, width), F32),
            pltpu.SMEM((supers, supers), jnp.int32),
            pltpu.VMEM((count, loads), BF16),
            pltpu.VMEM((ranks, rows, count), F32),
            pltpu.VMEM((ranks, rows, count), F32),
            pltpu.VMEM((2 * width, width), BF16),
            pltpu.VMEM((width, 3 * width), BF16),
            pltpu.VMEM((count, width), F32),
            pltpu.VMEM((count, width), BF16),
            pltpu.VMEM((supers, count, width), BF16),
            pltpu.VMEM((supers, count, width), BF16),
            pltpu.VMEM((supers, count, width), BF16),
            pltpu.VMEM((groups, rows, width), wire),
            pltpu.VMEM((groups, rows, width), wire),
            pltpu.VMEM((groups, rows, width), F32),
            pltpu.VMEM((groups, rows, width), wire),
            pltpu.VMEM((groups, rows, width), wire),
            dma((5,)), dma((zs,)), dma((zs, xs)), dma((zs, xs)), dma((ranks,)),
            dma((supers,)), dma((supers,)), dma((supers,)), dma((supers,)),
            dma, dma, dma((groups,)), dma((groups,)),
        ],
        compiler_params=pltpu.CompilerParams(
            collective_id=0, has_side_effects=True, vmem_limit_bytes=LIMIT
        ),
    )(*(
        pltpu.with_memory_space_constraint(value, pltpu.HBM)
        for value in (right_sides, stripe.T, inverses, structure, heater_wattages.T)
    ))
    return pl.pallas_call(
        write_out,
        out_shape=(
            jax.ShapeDtypeStruct((count, width), BF16),
            jax.ShapeDtypeStruct((rows, width), F32),
        ),
        in_specs=[vmem, vmem],
        out_specs=(whole, whole),
        scratch_shapes=[dma((2,))],
    )(solved, reply)


def solution(mesh):
    placed = (P("rhs", "fac"), P("fac", "rhs"), P("fac", None, None), P(), P(None, "rhs"))
    return jax.shard_map(
        body,
        mesh=mesh,
        in_specs=placed,
        out_specs=(P("rhs", "fac"), P("rhs", "fac")),
        check_vma=False,
    )
```

```python
import functools

import jax
import jax.numpy as jnp
from jax import lax
from jax.experimental import pallas as pl
from jax.experimental.pallas import tpu as pltpu
from jax.sharding import PartitionSpec as P

F32 = jnp.float32
BF16 = jnp.bfloat16
LIMIT = 32 * 1024 * 1024
NT = (((1,), (1,)), ((), ()))
NN = (((1,), (0,)), ((), ()))


def mul(left, right, dims):
    return lax.dot_general(left, right, dims, preferred_element_type=F32)


def split(value):
    high = value.astype(BF16)
    return high, (value - high.astype(F32)).astype(BF16)


def kernel(
    shape, sides_any, stripe_any, inverse_any, structure_any, watts_any, out_ref, reply_ref,
    factor, sides, inverse, keeps, watts_in, watts, watts_own, plain, turned, base, fwd, fwd_in,
    upd_out, upd_in, pair_out, pair_in, mine, sum_out, sum_in,
    load, z_send, x_send, c_send, factor_recv, f_send, f_recv, u_send, u_recv,
    pair_send, pair_recv, s_send, s_recv,
):
    supers, ranks, zs, xs = shape
    groups = ranks // 2
    width = inverse.shape[0]
    per = width // factor.shape[1]
    s = lax.axis_index("fac")
    me = lax.axis_index("rhs")
    core = lax.rem(me, 2)
    chip = lax.div(me, 2)
    x = lax.rem(chip, xs)
    z = lax.div(chip, xs)

    def rank(zz, xx, cc):
        return (zz * xs + xx) * 2 + cc

    def needed(b):
        return b < s * per

    barrier = pltpu.get_barrier_semaphore()
    pl.semaphore_signal(barrier, inc=1, device_id={"rhs": chip * 2 + 1 - core})
    for k in range(1, supers):
        pl.semaphore_signal(barrier, inc=1, device_id={"fac": lax.rem(s + k, supers)})
    for k in range(1, groups):
        pl.semaphore_signal(barrier, inc=1, device_id={"rhs": lax.rem(chip + k, groups) * 2 + core})
    loads = [
        pltpu.make_async_copy(stripe_any, factor.at[me], load.at[0]),
        pltpu.make_async_copy(inverse_any.at[0], inverse, load.at[1]),
        pltpu.make_async_copy(sides_any, sides, load.at[2]),
        pltpu.make_async_copy(watts_any, watts_in, load.at[3]),
        pltpu.make_async_copy(structure_any, keeps, load.at[4]),
    ]
    for copy in loads:
        copy.start()

    loads[0].wait()
    pl.semaphore_wait(barrier, groups + supers - 1)

    def factor_copy(b, send, where):
        return pltpu.make_async_remote_copy(
            src_ref=factor.at[b], dst_ref=factor.at[b], send_sem=send,
            recv_sem=factor_recv.at[b], device_id={"rhs": where},
        )

    def forward_copy(t, k, where):
        return pltpu.make_async_remote_copy(
            src_ref=fwd, dst_ref=fwd_in.at[t], send_sem=f_send.at[k],
            recv_sem=f_recv.at[t], device_id={"fac": where},
        )

    def update_copy(t, where):
        return pltpu.make_async_remote_copy(
            src_ref=upd_out.at[where], dst_ref=upd_in.at[t], send_sem=u_send.at[where],
            recv_sem=u_recv.at[t], device_id={"fac": where},
        )

    @pl.when(needed(me))
    def _():
        for zz in range(zs - 1, -1, -1):
            @pl.when(zz != z)
            def _():
                factor_copy(me, z_send.at[zz], rank(zz, x, core)).start()

    def relay(k):
        b = rank(lax.rem(z + zs - k, zs), x, core)

        @pl.when(needed(b))
        def _():
            if k > 0:
                factor_copy(b, z_send.at[0], me).wait_recv()
            for j in range(1, xs):
                factor_copy(b, x_send.at[k, j], rank(z, lax.rem(x + j, xs), core)).start()
            factor_copy(b, c_send.at[k, 0], rank(z, x, 1 - core)).start()

    relay(0)

    loads[1].wait()
    high, low = split(inverse[...])
    plain[:width] = high
    plain[width:] = low
    turned[:, :width] = high
    turned[:, width:2 * width] = low
    turned[:, 2 * width:] = high
    loads[2].wait()
    loads[4].wait()

    def twice(value):
        return jnp.concatenate([value, value], axis=1)

    def thrice(value):
        a_high, a_low = split(value)
        return jnp.concatenate([a_high, a_high, a_low], axis=1)

    @pl.when(s == 0)
    def _():
        fwd[...] = mul(twice(sides[...]), turned[:, :2 * width], NT).astype(BF16)
        for k in range(1, supers):
            forward_copy(0, k, k).start()

    for k in range(1, zs):
        relay(k)
    for k in range(zs):
        for j in range(1, xs):
            b = rank(lax.rem(z + zs - k, zs), lax.rem(x + xs - j, xs), core)

            @pl.when(needed(b))
            def _():
                factor_copy(b, z_send.at[0], me).wait_recv()
                factor_copy(b, c_send.at[k, j], rank(z, x, 1 - core)).start()

    loads[3].wait()
    watts[...] = watts_in[...].astype(F32).T.reshape(watts.shape)
    for g in range(groups):
        watts_own[g] = watts[2 * g + 1 - core]
        watts_own[groups + g] = watts[2 * g + core]

    for zz in range(zs):
        for xx in range(xs):
            b = rank(zz, xx, 1 - core)

            @pl.when(needed(b))
            def _():
                factor_copy(b, z_send.at[0], me).wait_recv()

    def block(t):
        return factor[t * per:(t + 1) * per].reshape(width, width)

    @pl.when(s > 0)
    def _():
        base[...] = sides[...].astype(F32)
        for t in range(supers - 1):
            @pl.when(s > t)
            def _():
                forward_copy(t, 0, s).wait_recv()
                keep = keeps[s, t].astype(F32)
                base[...] -= keep * mul(fwd_in[t], block(t), NN)
        fwd[...] = mul(thrice(base[...]), turned[...], NT).astype(BF16)
        for k in range(2, supers):
            @pl.when(s < k)
            def _():
                forward_copy(s, k, k).start()

    base[...] = mul(twice(fwd[...]), plain[...], NN)
    out_ref[...] = base[...].astype(BF16)
    for t in range(supers - 1, 0, -1):
        @pl.when(s < t)
        def _():
            update_copy(t, s).wait_recv()
            base[...] -= mul(twice(upd_in[t]), plain[...], NN)
            if t - 1 == 0:
                out_ref[...] = base[...].astype(BF16)
            else:
                @pl.when(s == t - 1)
                def _():
                    out_ref[...] = base[...].astype(BF16)
    for t in range(supers - 2, -1, -1):
        @pl.when(s > t)
        def _():
            keep = keeps[s, t].astype(F32)
            upd_out[t] = (keep * mul(out_ref[...], block(t), NT)).astype(BF16)
            update_copy(s, t).start()

    def product(first):
        rows = watts_own[first:first + groups]
        rows = rows.reshape(groups * rows.shape[1], rows.shape[2]).astype(BF16)
        return mul(rows, out_ref[...], NN).reshape(mine.shape)

    pair_out[...] = product(0).astype(pair_out.dtype)
    pair = pltpu.make_async_remote_copy(
        src_ref=pair_out, dst_ref=pair_in, send_sem=pair_send, recv_sem=pair_recv,
        device_id={"rhs": rank(z, x, 1 - core)},
    )
    pair.start()
    mine[...] = product(groups)
    pair.wait_recv()
    both = mine[...] + pair_in[...].astype(F32)
    mine[...] = both
    sum_out[...] = both.astype(sum_out.dtype)

    def sum_copy(target, source, k):
        return pltpu.make_async_remote_copy(
            src_ref=sum_out.at[target], dst_ref=sum_in.at[source], send_sem=s_send.at[k],
            recv_sem=s_recv.at[source], device_id={"rhs": target * 2 + core},
        )

    for k in range(1, groups):
        sum_copy(lax.rem(chip + k, groups), chip, k).start()
    total = mine[chip]
    for k in range(1, groups):
        source = lax.rem(chip + groups - k, groups)
        sum_copy(chip, source, 0).wait_recv()
        total = total + sum_in[source].astype(F32)
    reply_ref[...] = total

    for k in range(1, groups):
        sum_copy(lax.rem(chip + k, groups), chip, k).wait_send()
    pair.wait_send()
    for t in range(supers - 1):
        @pl.when(s > t)
        def _():
            update_copy(s, t).wait_send()
    for k in range(1, supers):
        @pl.when(s < k)
        def _():
            forward_copy(s, k, k).wait_send()

    @pl.when(needed(me))
    def _():
        for zz in range(zs):
            @pl.when(zz != z)
            def _():
                factor_copy(me, z_send.at[zz], me).wait_send()
    for k in range(zs):
        own = rank(lax.rem(z + zs - k, zs), x, core)

        @pl.when(needed(own))
        def _():
            factor_copy(own, c_send.at[k, 0], me).wait_send()
            for j in range(1, xs):
                factor_copy(own, x_send.at[k, j], me).wait_send()
        for j in range(1, xs):
            b = rank(lax.rem(z + zs - k, zs), lax.rem(x + xs - j, xs), core)

            @pl.when(needed(b))
            def _():
                factor_copy(b, c_send.at[k, j], me).wait_send()


def write_out(solved_ref, reply_ref, solved_out, reply_out, sem):
    first = pltpu.make_async_copy(solved_ref, solved_out, sem.at[0])
    second = pltpu.make_async_copy(reply_ref, reply_out, sem.at[1])
    first.start()
    second.start()
    first.wait()
    second.wait()


def body(right_sides, stripe, inverses, structure, heater_wattages):
    supers = lax.axis_size("fac")
    ranks = lax.axis_size("rhs")
    zs = 4
    xs = ranks // (2 * zs)
    count, width = right_sides.shape
    columns = stripe.shape[1]
    loads = heater_wattages.shape[0]
    rows = loads // ranks
    groups = ranks // 2
    wire = BF16 if rows % 16 == 0 else F32
    dma = pltpu.SemaphoreType.DMA
    vmem = pl.BlockSpec(memory_space=pltpu.VMEM)
    whole = pl.BlockSpec(memory_space=pl.ANY)
    solved, reply = pl.pallas_call(
        functools.partial(kernel, (supers, ranks, zs, xs)),
        out_shape=(
            pltpu.VMEM((count, width), BF16),
            pltpu.VMEM((rows, width), F32),
        ),
        in_specs=[whole] * 5,
        out_specs=(vmem, vmem),
        scratch_shapes=[
            pltpu.VMEM((ranks, columns, width), BF16),
            pltpu.VMEM((count, width), BF16),
            pltpu.VMEM((width, width), F32),
            pltpu.SMEM((supers, supers), jnp.int32),
            pltpu.VMEM((count, loads), BF16),
            pltpu.VMEM((ranks, rows, count), F32),
            pltpu.VMEM((ranks, rows, count), F32),
            pltpu.VMEM((2 * width, width), BF16),
            pltpu.VMEM((width, 3 * width), BF16),
            pltpu.VMEM((count, width), F32),
            pltpu.VMEM((count, width), BF16),
            pltpu.VMEM((supers, count, width), BF16),
            pltpu.VMEM((supers, count, width), BF16),
            pltpu.VMEM((supers, count, width), BF16),
            pltpu.VMEM((groups, rows, width), wire),
            pltpu.VMEM((groups, rows, width), wire),
            pltpu.VMEM((groups, rows, width), F32),
            pltpu.VMEM((groups, rows, width), wire),
            pltpu.VMEM((groups, rows, width), wire),
            dma((5,)), dma((zs,)), dma((zs, xs)), dma((zs, xs)), dma((ranks,)),
            dma((supers,)), dma((supers,)), dma((supers,)), dma((supers,)),
            dma, dma, dma((groups,)), dma((groups,)),
        ],
        compiler_params=pltpu.CompilerParams(
            collective_id=0, has_side_effects=True, vmem_limit_bytes=LIMIT
        ),
    )(*(
        pltpu.with_memory_space_constraint(value, pltpu.HBM)
        for value in (right_sides, stripe.T, inverses, structure, heater_wattages.T)
    ))
    return pl.pallas_call(
        write_out,
        out_shape=(
            jax.ShapeDtypeStruct((count, width), BF16),
            jax.ShapeDtypeStruct((rows, width), F32),
        ),
        in_specs=[vmem, vmem],
        out_specs=(whole, whole),
        scratch_shapes=[dma((2,))],
    )(
        pltpu.with_memory_space_constraint(solved, pltpu.VMEM),
        pltpu.with_memory_space_constraint(reply, pltpu.VMEM),
    )


def solution(mesh):
    placed = (P("rhs", "fac"), P("fac", "rhs"), P("fac", None, None), P(), P(None, "rhs"))
    return jax.shard_map(
        body,
        mesh=mesh,
        in_specs=placed,
        out_specs=(P("rhs", "fac"), P("rhs", "fac")),
        check_vma=False,
    )
```

```python
import functools

import jax
import jax.numpy as jnp
from jax import lax
from jax.experimental import pallas as pl
from jax.experimental.pallas import tpu as pltpu
from jax.sharding import PartitionSpec as P

F32 = jnp.float32
BF16 = jnp.bfloat16
LIMIT = 32 * 1024 * 1024
NT = (((1,), (1,)), ((), ()))
NN = (((1,), (0,)), ((), ()))


def mul(left, right, dims):
    return lax.dot_general(left, right, dims, preferred_element_type=F32)


def split(value):
    high = value.astype(BF16)
    return high, (value - high.astype(F32)).astype(BF16)


def kernel(
    shape, sides_any, stripe_any, inverse_any, structure_any, watts_any, out_ref, reply_ref,
    factor, sides, inverse, keeps, watts_in, watts, watts_own, plain, turned, base, fwd, fwd_in,
    upd_out_a, upd_out_b, upd_in_a, upd_in_b, pair_out, pair_in, mine, sum_out, sum_in,
    load, z_send, x_send, c_send, factor_recv, f_send, f_recv, u_send, u_recv,
    pair_send, pair_recv, s_send, s_recv,
):
    supers, ranks, zs, xs = shape
    groups = ranks // 2
    width = inverse.shape[0]
    per = width // factor.shape[1]
    s = lax.axis_index("fac")
    me = lax.axis_index("rhs")
    core = lax.rem(me, 2)
    chip = lax.div(me, 2)
    x = lax.rem(chip, xs)
    z = lax.div(chip, xs)

    def rank(zz, xx, cc):
        return (zz * xs + xx) * 2 + cc

    def needed(b):
        return b < s * per

    barrier = pltpu.get_barrier_semaphore()
    pl.semaphore_signal(barrier, inc=1, device_id={"rhs": chip * 2 + 1 - core})
    for k in range(1, supers):
        pl.semaphore_signal(barrier, inc=1, device_id={"fac": lax.rem(s + k, supers)})
    for k in range(1, groups):
        pl.semaphore_signal(barrier, inc=1, device_id={"rhs": lax.rem(chip + k, groups) * 2 + core})
    loads = [
        pltpu.make_async_copy(stripe_any, factor.at[me], load.at[0]),
        pltpu.make_async_copy(inverse_any.at[0], inverse, load.at[1]),
        pltpu.make_async_copy(sides_any, sides, load.at[2]),
        pltpu.make_async_copy(watts_any, watts_in, load.at[3]),
        pltpu.make_async_copy(structure_any, keeps, load.at[4]),
    ]
    for copy in loads:
        copy.start()

    loads[0].wait()
    pl.semaphore_wait(barrier, groups + supers - 1)

    def factor_copy(b, send, where):
        return pltpu.make_async_remote_copy(
            src_ref=factor.at[b], dst_ref=factor.at[b], send_sem=send,
            recv_sem=factor_recv.at[b], device_id={"rhs": where},
        )

    def forward_copy(t, k, where):
        return pltpu.make_async_remote_copy(
            src_ref=fwd, dst_ref=fwd_in.at[t], send_sem=f_send.at[k],
            recv_sem=f_recv.at[t], device_id={"fac": where},
        )

    cuts = ((upd_out_a, upd_in_a, 0, 256), (upd_out_b, upd_in_b, 256, width))

    def update_copy(t, where, half):
        return pltpu.make_async_remote_copy(
            src_ref=cuts[half][0].at[where], dst_ref=cuts[half][1].at[t],
            send_sem=u_send.at[where, half], recv_sem=u_recv.at[t, half],
            device_id={"fac": where},
        )

    @pl.when(needed(me))
    def _():
        for zz in range(zs - 1, -1, -1):
            @pl.when(zz != z)
            def _():
                factor_copy(me, z_send.at[zz], rank(zz, x, core)).start()

    def relay(k):
        b = rank(lax.rem(z + zs - k, zs), x, core)

        @pl.when(needed(b))
        def _():
            if k > 0:
                factor_copy(b, z_send.at[0], me).wait_recv()
            for j in range(1, xs):
                factor_copy(b, x_send.at[k, j], rank(z, lax.rem(x + j, xs), core)).start()
            factor_copy(b, c_send.at[k, 0], rank(z, x, 1 - core)).start()

    relay(0)

    loads[1].wait()
    high, low = split(inverse[...])
    plain[:width] = high
    plain[width:] = low
    turned[:, :width] = high
    turned[:, width:] = low
    loads[2].wait()
    loads[4].wait()

    def twice(value):
        return jnp.concatenate([value, value], axis=1)

    @pl.when(s == 0)
    def _():
        fwd[...] = mul(twice(sides[...]), turned[...], NT).astype(BF16)
        for k in range(1, supers):
            forward_copy(0, k, k).start()

    for k in range(1, zs):
        relay(k)
    for k in range(zs):
        for j in range(1, xs):
            b = rank(lax.rem(z + zs - k, zs), lax.rem(x + xs - j, xs), core)

            @pl.when(needed(b))
            def _():
                factor_copy(b, z_send.at[0], me).wait_recv()
                factor_copy(b, c_send.at[k, j], rank(z, x, 1 - core)).start()

    loads[3].wait()
    watts[...] = watts_in[...].astype(F32).T.reshape(watts.shape)
    for g in range(groups):
        watts_own[g] = watts[2 * g + 1 - core]
        watts_own[groups + g] = watts[2 * g + core]

    for zz in range(zs):
        for xx in range(xs):
            b = rank(zz, xx, 1 - core)

            @pl.when(needed(b))
            def _():
                factor_copy(b, z_send.at[0], me).wait_recv()

    def block(t):
        return factor[t * per:(t + 1) * per].reshape(width, width)

    @pl.when(s > 0)
    def _():
        base[...] = sides[...].astype(F32)
        for t in range(supers - 1):
            @pl.when(s > t)
            def _():
                forward_copy(t, 0, s).wait_recv()
                keep = keeps[s, t].astype(F32)
                base[...] -= keep * mul(fwd_in[t], block(t), NN)
        fwd[...] = mul(twice(base[...].astype(BF16)), turned[...], NT).astype(BF16)
        for k in range(2, supers):
            @pl.when(s < k)
            def _():
                forward_copy(s, k, k).start()

    base[...] = mul(twice(fwd[...]), plain[...], NN)
    out_ref[...] = base[...].astype(BF16)
    for t in range(supers - 1, 0, -1):
        @pl.when(s < t)
        def _():
            for half, (_, arrived, first, end) in enumerate(cuts):
                update_copy(t, s, half).wait_recv()
                base[...] -= mul(arrived[t], plain[first:end], NN)
            if t - 1 == 0:
                out_ref[...] = base[...].astype(BF16)
            else:
                @pl.when(s == t - 1)
                def _():
                    out_ref[...] = base[...].astype(BF16)
    for t in range(supers - 2, -1, -1):
        @pl.when(s > t)
        def _():
            keep = keeps[s, t].astype(F32)
            for half, (leaving, _, first, end) in enumerate(cuts):
                rows = block(t)[first:end]
                leaving[t] = (keep * mul(out_ref[...], rows, NT)).astype(BF16)
                update_copy(s, t, half).start()

    def product(first):
        rows = watts_own[first:first + groups]
        rows = rows.reshape(groups * rows.shape[1], rows.shape[2]).astype(BF16)
        return mul(rows, out_ref[...], NN).reshape(mine.shape)

    pair_out[...] = product(0).astype(pair_out.dtype)
    pair = pltpu.make_async_remote_copy(
        src_ref=pair_out, dst_ref=pair_in, send_sem=pair_send, recv_sem=pair_recv,
        device_id={"rhs": rank(z, x, 1 - core)},
    )
    pair.start()
    mine[...] = product(groups)
    pair.wait_recv()
    both = mine[...] + pair_in[...].astype(F32)
    mine[...] = both
    sum_out[...] = both.astype(sum_out.dtype)

    def sum_copy(target, source, k):
        return pltpu.make_async_remote_copy(
            src_ref=sum_out.at[target], dst_ref=sum_in.at[source], send_sem=s_send.at[k],
            recv_sem=s_recv.at[source], device_id={"rhs": target * 2 + core},
        )

    step = jnp.where(2 * z >= zs, 1, groups - 1)
    for k in range(1, groups):
        sum_copy(lax.rem(chip + k * step, groups), chip, k).start()
    total = mine[chip]
    for k in range(1, groups):
        source = lax.rem(chip + groups - k, groups)
        sum_copy(chip, source, 0).wait_recv()
        total = total + sum_in[source].astype(F32)
    reply_ref[...] = total

    for k in range(1, groups):
        sum_copy(lax.rem(chip + k * step, groups), chip, k).wait_send()
    pair.wait_send()
    for t in range(supers - 1):
        @pl.when(s > t)
        def _():
            for half in range(2):
                update_copy(s, t, half).wait_send()
    for k in range(1, supers):
        @pl.when(s < k)
        def _():
            forward_copy(s, k, k).wait_send()

    @pl.when(needed(me))
    def _():
        for zz in range(zs):
            @pl.when(zz != z)
            def _():
                factor_copy(me, z_send.at[zz], me).wait_send()
    for k in range(zs):
        own = rank(lax.rem(z + zs - k, zs), x, core)

        @pl.when(needed(own))
        def _():
            factor_copy(own, c_send.at[k, 0], me).wait_send()
            for j in range(1, xs):
                factor_copy(own, x_send.at[k, j], me).wait_send()
        for j in range(1, xs):
            b = rank(lax.rem(z + zs - k, zs), lax.rem(x + xs - j, xs), core)

            @pl.when(needed(b))
            def _():
                factor_copy(b, c_send.at[k, j], me).wait_send()


def write_out(solved_ref, reply_ref, solved_out, reply_out, sem):
    first = pltpu.make_async_copy(solved_ref, solved_out, sem.at[0])
    second = pltpu.make_async_copy(reply_ref, reply_out, sem.at[1])
    first.start()
    second.start()
    first.wait()
    second.wait()


def body(right_sides, stripe, inverses, structure, heater_wattages):
    supers = lax.axis_size("fac")
    ranks = lax.axis_size("rhs")
    zs = 4
    xs = ranks // (2 * zs)
    count, width = right_sides.shape
    columns = stripe.shape[1]
    loads = heater_wattages.shape[0]
    rows = loads // ranks
    groups = ranks // 2
    wire = BF16 if rows % 16 == 0 else F32
    dma = pltpu.SemaphoreType.DMA
    vmem = pl.BlockSpec(memory_space=pltpu.VMEM)
    whole = pl.BlockSpec(memory_space=pl.ANY)
    solved, reply = pl.pallas_call(
        functools.partial(kernel, (supers, ranks, zs, xs)),
        out_shape=(
            pltpu.VMEM((count, width), BF16),
            pltpu.VMEM((rows, width), F32),
        ),
        in_specs=[whole] * 5,
        out_specs=(vmem, vmem),
        scratch_shapes=[
            pltpu.VMEM((ranks, columns, width), BF16),
            pltpu.VMEM((count, width), BF16),
            pltpu.VMEM((width, width), F32),
            pltpu.SMEM((supers, supers), jnp.int32),
            pltpu.VMEM((count, loads), BF16),
            pltpu.VMEM((ranks, rows, count), F32),
            pltpu.VMEM((ranks, rows, count), F32),
            pltpu.VMEM((2 * width, width), BF16),
            pltpu.VMEM((width, 2 * width), BF16),
            pltpu.VMEM((count, width), F32),
            pltpu.VMEM((count, width), BF16),
            pltpu.VMEM((supers, count, width), BF16),
            pltpu.VMEM((supers, count, 256), BF16),
            pltpu.VMEM((supers, count, width - 256), BF16),
            pltpu.VMEM((supers, count, 256), BF16),
            pltpu.VMEM((supers, count, width - 256), BF16),
            pltpu.VMEM((groups, rows, width), wire),
            pltpu.VMEM((groups, rows, width), wire),
            pltpu.VMEM((groups, rows, width), F32),
            pltpu.VMEM((groups, rows, width), wire),
            pltpu.VMEM((groups, rows, width), wire),
            dma((5,)), dma((zs,)), dma((zs, xs)), dma((zs, xs)), dma((ranks,)),
            dma((supers,)), dma((supers,)), dma((supers, 2)), dma((supers, 2)),
            dma, dma, dma((groups,)), dma((groups,)),
        ],
        compiler_params=pltpu.CompilerParams(
            collective_id=0, has_side_effects=True, vmem_limit_bytes=LIMIT
        ),
    )(*(
        pltpu.with_memory_space_constraint(value, pltpu.HBM)
        for value in (right_sides, stripe.T, inverses, structure, heater_wattages.T)
    ))
    return pl.pallas_call(
        write_out,
        out_shape=(
            jax.ShapeDtypeStruct((count, width), BF16),
            jax.ShapeDtypeStruct((rows, width), F32),
        ),
        in_specs=[vmem, vmem],
        out_specs=(whole, whole),
        scratch_shapes=[dma((2,))],
    )(
        pltpu.with_memory_space_constraint(solved, pltpu.VMEM),
        pltpu.with_memory_space_constraint(reply, pltpu.VMEM),
    )


def solution(mesh):
    placed = (P("rhs", "fac"), P("fac", "rhs"), P("fac", None, None), P(), P(None, "rhs"))
    return jax.shard_map(
        body,
        mesh=mesh,
        in_specs=placed,
        out_specs=(P("rhs", "fac"), P("rhs", "fac")),
        check_vma=False,
    )
```

```python
import functools

import jax
import jax.numpy as jnp
from jax import lax
from jax.experimental import pallas as pl
from jax.experimental.pallas import tpu as pltpu
from jax.sharding import PartitionSpec as P

F32 = jnp.float32
BF16 = jnp.bfloat16
LIMIT = 32 * 1024 * 1024
NT = (((1,), (1,)), ((), ()))
NN = (((1,), (0,)), ((), ()))


def mul(left, right, dims):
    return lax.dot_general(left, right, dims, preferred_element_type=F32)


def split(value):
    high = value.astype(BF16)
    return high, (value - high.astype(F32)).astype(BF16)


def kernel(
    shape, sides_any, stripe_any, inverse_any, structure_any, watts_any, out_ref, reply_ref,
    factor, sides, inverse, keeps, watts_in, watts, watts_own, plain, turned, base, fwd, fwd_in,
    upd_out_a, upd_out_b, upd_in_a, upd_in_b, pair_out, pair_in, mine, sum_out, sum_in,
    load, z_send, z_pass, x_send, c_send, factor_recv, f_send, f_recv, u_send, u_recv,
    pair_send, pair_recv, s_send, s_recv,
):
    supers, ranks, zs, xs = shape
    groups = ranks // 2
    width = inverse.shape[0]
    per = width // factor.shape[1]
    s = lax.axis_index("fac")
    me = lax.axis_index("rhs")
    core = lax.rem(me, 2)
    chip = lax.div(me, 2)
    x = lax.rem(chip, xs)
    z = lax.div(chip, xs)

    def rank(zz, xx, cc):
        return (zz * xs + xx) * 2 + cc

    def needed(b):
        return b < s * per

    barrier = pltpu.get_barrier_semaphore()
    pl.semaphore_signal(barrier, inc=1, device_id={"rhs": chip * 2 + 1 - core})
    for k in range(1, supers):
        pl.semaphore_signal(barrier, inc=1, device_id={"fac": lax.rem(s + k, supers)})
    for k in range(1, groups):
        pl.semaphore_signal(barrier, inc=1, device_id={"rhs": lax.rem(chip + k, groups) * 2 + core})
    loads = [
        pltpu.make_async_copy(stripe_any, factor.at[me], load.at[0]),
        pltpu.make_async_copy(inverse_any.at[0], inverse, load.at[1]),
        pltpu.make_async_copy(sides_any, sides, load.at[2]),
        pltpu.make_async_copy(watts_any, watts_in, load.at[3]),
        pltpu.make_async_copy(structure_any, keeps, load.at[4]),
    ]
    for copy in loads:
        copy.start()

    loads[0].wait()
    pl.semaphore_wait(barrier, groups + supers - 1)

    def factor_copy(b, send, where):
        return pltpu.make_async_remote_copy(
            src_ref=factor.at[b], dst_ref=factor.at[b], send_sem=send,
            recv_sem=factor_recv.at[b], device_id={"rhs": where},
        )

    def forward_copy(t, k, where):
        return pltpu.make_async_remote_copy(
            src_ref=fwd, dst_ref=fwd_in.at[t], send_sem=f_send.at[k],
            recv_sem=f_recv.at[t], device_id={"fac": where},
        )

    cuts = ((upd_out_a, upd_in_a, 0, 256), (upd_out_b, upd_in_b, 256, width))

    def update_copy(t, where, half):
        return pltpu.make_async_remote_copy(
            src_ref=cuts[half][0].at[where], dst_ref=cuts[half][1].at[t],
            send_sem=u_send.at[where, half], recv_sem=u_recv.at[t, half],
            device_id={"fac": where},
        )

    def direct(zz):
        far_low = (2 * z >= zs) & (zz == 0)
        far_high = (2 * z < zs) & (zz == zs - 1)
        return (zz != z) & ~far_low & ~far_high

    def passed_on(zz):
        to_high = (z == zs - 2) & (2 * zz < zs)
        to_low = (z == 1) & (2 * zz >= zs)
        return to_high | to_low

    end = jnp.where(z == 1, 0, zs - 1)

    @pl.when(needed(me))
    def _():
        for zz in range(zs - 1, -1, -1):
            @pl.when(direct(zz))
            def _():
                factor_copy(me, z_send.at[zz], rank(zz, x, core)).start()

    def relay(k):
        zz = lax.rem(z + zs - k, zs)
        b = rank(zz, x, core)

        @pl.when(needed(b))
        def _():
            if k > 0:
                factor_copy(b, z_send.at[0], me).wait_recv()

                @pl.when(passed_on(zz))
                def _():
                    factor_copy(b, z_pass.at[k], rank(end, x, core)).start()
            for j in range(1, xs):
                factor_copy(b, x_send.at[k, j], rank(z, lax.rem(x + j, xs), core)).start()
            factor_copy(b, c_send.at[k, 0], rank(z, x, 1 - core)).start()

    relay(0)

    loads[1].wait()
    high, low = split(inverse[...])
    plain[:width] = high
    plain[width:] = low
    turned[:, :width] = high
    turned[:, width:] = low
    loads[2].wait()
    loads[4].wait()

    def twice(value):
        return jnp.concatenate([value, value], axis=1)

    @pl.when(s == 0)
    def _():
        fwd[...] = mul(twice(sides[...]), turned[...], NT).astype(BF16)
        for k in range(1, supers):
            forward_copy(0, k, k).start()

    for k in range(1, zs):
        relay(k)
    for k in range(zs):
        for j in range(1, xs):
            b = rank(lax.rem(z + zs - k, zs), lax.rem(x + xs - j, xs), core)

            @pl.when(needed(b))
            def _():
                factor_copy(b, z_send.at[0], me).wait_recv()
                factor_copy(b, c_send.at[k, j], rank(z, x, 1 - core)).start()

    loads[3].wait()
    watts[...] = watts_in[...].astype(F32).T.reshape(watts.shape)
    for g in range(groups):
        watts_own[g] = watts[2 * g + 1 - core]
        watts_own[groups + g] = watts[2 * g + core]

    for zz in range(zs):
        for xx in range(xs):
            b = rank(zz, xx, 1 - core)

            @pl.when(needed(b))
            def _():
                factor_copy(b, z_send.at[0], me).wait_recv()

    def block(t):
        return factor[t * per:(t + 1) * per].reshape(width, width)

    @pl.when(s > 0)
    def _():
        base[...] = sides[...].astype(F32)
        for t in range(supers - 1):
            @pl.when(s > t)
            def _():
                forward_copy(t, 0, s).wait_recv()
                keep = keeps[s, t].astype(F32)
                base[...] -= keep * mul(fwd_in[t], block(t), NN)
        fwd[...] = mul(twice(base[...].astype(BF16)), turned[...], NT).astype(BF16)
        for k in range(2, supers):
            @pl.when(s < k)
            def _():
                forward_copy(s, k, k).start()

    base[...] = mul(twice(fwd[...]), plain[...], NN)
    out_ref[...] = base[...].astype(BF16)
    for t in range(supers - 1, 0, -1):
        @pl.when(s < t)
        def _():
            for half, (_, arrived, first, last) in enumerate(cuts):
                update_copy(t, s, half).wait_recv()
                base[...] -= mul(arrived[t], plain[first:last], NN)
            if t - 1 == 0:
                out_ref[...] = base[...].astype(BF16)
            else:
                @pl.when(s == t - 1)
                def _():
                    out_ref[...] = base[...].astype(BF16)
    for t in range(supers - 2, -1, -1):
        @pl.when(s > t)
        def _():
            keep = keeps[s, t].astype(F32)
            for half, (leaving, _, first, last) in enumerate(cuts):
                rows = block(t)[first:last]
                leaving[t] = (keep * mul(out_ref[...], rows, NT)).astype(BF16)
                update_copy(s, t, half).start()

    def product(first):
        rows = watts_own[first:first + groups]
        rows = rows.reshape(groups * rows.shape[1], rows.shape[2]).astype(BF16)
        return mul(rows, out_ref[...], NN).reshape(mine.shape)

    pair_out[...] = product(0).astype(pair_out.dtype)
    pair = pltpu.make_async_remote_copy(
        src_ref=pair_out, dst_ref=pair_in, send_sem=pair_send, recv_sem=pair_recv,
        device_id={"rhs": rank(z, x, 1 - core)},
    )
    pair.start()
    mine[...] = product(groups)
    pair.wait_recv()
    both = mine[...] + pair_in[...].astype(F32)
    mine[...] = both
    sum_out[...] = both.astype(sum_out.dtype)

    def sum_copy(target, source, k):
        return pltpu.make_async_remote_copy(
            src_ref=sum_out.at[target], dst_ref=sum_in.at[source], send_sem=s_send.at[k],
            recv_sem=s_recv.at[source], device_id={"rhs": target * 2 + core},
        )

    step = jnp.where(2 * z >= zs, 1, groups - 1)
    for k in range(1, groups):
        sum_copy(lax.rem(chip + k * step, groups), chip, k).start()
    total = mine[chip]
    for k in range(1, groups):
        source = lax.rem(chip + groups - k, groups)
        sum_copy(chip, source, 0).wait_recv()
        total = total + sum_in[source].astype(F32)
    reply_ref[...] = total

    for k in range(1, groups):
        sum_copy(lax.rem(chip + k * step, groups), chip, k).wait_send()
    pair.wait_send()
    for t in range(supers - 1):
        @pl.when(s > t)
        def _():
            for half in range(2):
                update_copy(s, t, half).wait_send()
    for k in range(1, supers):
        @pl.when(s < k)
        def _():
            forward_copy(s, k, k).wait_send()

    @pl.when(needed(me))
    def _():
        for zz in range(zs):
            @pl.when(direct(zz))
            def _():
                factor_copy(me, z_send.at[zz], me).wait_send()
    for k in range(zs):
        zz = lax.rem(z + zs - k, zs)
        own = rank(zz, x, core)

        @pl.when(needed(own))
        def _():
            if k > 0:
                @pl.when(passed_on(zz))
                def _():
                    factor_copy(own, z_pass.at[k], me).wait_send()
            factor_copy(own, c_send.at[k, 0], me).wait_send()
            for j in range(1, xs):
                factor_copy(own, x_send.at[k, j], me).wait_send()
        for j in range(1, xs):
            b = rank(lax.rem(z + zs - k, zs), lax.rem(x + xs - j, xs), core)

            @pl.when(needed(b))
            def _():
                factor_copy(b, c_send.at[k, j], me).wait_send()


def write_out(solved_ref, reply_ref, solved_out, reply_out, sem):
    first = pltpu.make_async_copy(solved_ref, solved_out, sem.at[0])
    second = pltpu.make_async_copy(reply_ref, reply_out, sem.at[1])
    first.start()
    second.start()
    first.wait()
    second.wait()


def body(right_sides, stripe, inverses, structure, heater_wattages):
    supers = lax.axis_size("fac")
    ranks = lax.axis_size("rhs")
    zs = 4
    xs = ranks // (2 * zs)
    count, width = right_sides.shape
    columns = stripe.shape[1]
    loads = heater_wattages.shape[0]
    rows = loads // ranks
    groups = ranks // 2
    wire = BF16 if rows % 16 == 0 else F32
    dma = pltpu.SemaphoreType.DMA
    vmem = pl.BlockSpec(memory_space=pltpu.VMEM)
    whole = pl.BlockSpec(memory_space=pl.ANY)
    solved, reply = pl.pallas_call(
        functools.partial(kernel, (supers, ranks, zs, xs)),
        out_shape=(
            pltpu.VMEM((count, width), BF16),
            pltpu.VMEM((rows, width), F32),
        ),
        in_specs=[whole] * 5,
        out_specs=(vmem, vmem),
        scratch_shapes=[
            pltpu.VMEM((ranks, columns, width), BF16),
            pltpu.VMEM((count, width), BF16),
            pltpu.VMEM((width, width), F32),
            pltpu.SMEM((supers, supers), jnp.int32),
            pltpu.VMEM((count, loads), BF16),
            pltpu.VMEM((ranks, rows, count), F32),
            pltpu.VMEM((ranks, rows, count), F32),
            pltpu.VMEM((2 * width, width), BF16),
            pltpu.VMEM((width, 2 * width), BF16),
            pltpu.VMEM((count, width), F32),
            pltpu.VMEM((count, width), BF16),
            pltpu.VMEM((supers, count, width), BF16),
            pltpu.VMEM((supers, count, 256), BF16),
            pltpu.VMEM((supers, count, width - 256), BF16),
            pltpu.VMEM((supers, count, 256), BF16),
            pltpu.VMEM((supers, count, width - 256), BF16),
            pltpu.VMEM((groups, rows, width), wire),
            pltpu.VMEM((groups, rows, width), wire),
            pltpu.VMEM((groups, rows, width), F32),
            pltpu.VMEM((groups, rows, width), wire),
            pltpu.VMEM((groups, rows, width), wire),
            dma((5,)), dma((zs,)), dma((zs,)), dma((zs, xs)), dma((zs, xs)), dma((ranks,)),
            dma((supers,)), dma((supers,)), dma((supers, 2)), dma((supers, 2)),
            dma, dma, dma((groups,)), dma((groups,)),
        ],
        compiler_params=pltpu.CompilerParams(
            collective_id=0, has_side_effects=True, vmem_limit_bytes=LIMIT
        ),
    )(*(
        pltpu.with_memory_space_constraint(value, pltpu.HBM)
        for value in (right_sides, stripe.T, inverses, structure, heater_wattages.T)
    ))
    return pl.pallas_call(
        write_out,
        out_shape=(
            jax.ShapeDtypeStruct((count, width), BF16),
            jax.ShapeDtypeStruct((rows, width), F32),
        ),
        in_specs=[vmem, vmem],
        out_specs=(whole, whole),
        scratch_shapes=[dma((2,))],
    )(
        pltpu.with_memory_space_constraint(solved, pltpu.VMEM),
        pltpu.with_memory_space_constraint(reply, pltpu.VMEM),
    )


def solution(mesh):
    placed = (P("rhs", "fac"), P("fac", "rhs"), P("fac", None, None), P(), P(None, "rhs"))
    return jax.shard_map(
        body,
        mesh=mesh,
        in_specs=placed,
        out_specs=(P("rhs", "fac"), P("rhs", "fac")),
        check_vma=False,
    )
```

```python
import functools

import jax
import jax.numpy as jnp
from jax import lax
from jax.experimental import pallas as pl
from jax.experimental.pallas import tpu as pltpu
from jax.sharding import PartitionSpec as P

F32 = jnp.float32
BF16 = jnp.bfloat16
LIMIT = 32 * 1024 * 1024
NT = (((1,), (1,)), ((), ()))
NN = (((1,), (0,)), ((), ()))


def mul(left, right, dims):
    return lax.dot_general(left, right, dims, preferred_element_type=F32)


def split(value):
    high = value.astype(BF16)
    return high, (value - high.astype(F32)).astype(BF16)


def kernel(
    shape, sides_any, stripe_any, inverse_any, structure_any, watts_any, out_ref, reply_ref,
    factor, sides, inverse, keeps, watts_in, watts, watts_own, plain, turned, base, fwd, fwd_in,
    upd_out_a, upd_out_b, upd_in_a, upd_in_b, pair_out, pair_in, mine, sum_out, sum_in,
    load, z_send, x_send, c_send, factor_recv, f_send, f_recv, u_send, u_recv,
    pair_send, pair_recv, s_send, s_recv,
):
    supers, ranks, zs, xs = shape
    groups = ranks // 2
    width = inverse.shape[0]
    per = width // factor.shape[1]
    s = lax.axis_index("fac")
    me = lax.axis_index("rhs")
    core = lax.rem(me, 2)
    chip = lax.div(me, 2)
    x = lax.rem(chip, xs)
    z = lax.div(chip, xs)

    def rank(zz, xx, cc):
        return (zz * xs + xx) * 2 + cc

    def needed(b):
        return b < s * per

    barrier = pltpu.get_barrier_semaphore()
    pl.semaphore_signal(barrier, inc=1, device_id={"rhs": chip * 2 + 1 - core})
    for j in range(1, xs):
        beside = rank(z, lax.rem(x + j, xs), 1 - core)
        pl.semaphore_signal(barrier, inc=1, device_id={"rhs": beside})
    for k in range(1, supers):
        pl.semaphore_signal(barrier, inc=1, device_id={"fac": lax.rem(s + k, supers)})
    for k in range(1, groups):
        pl.semaphore_signal(barrier, inc=1, device_id={"rhs": lax.rem(chip + k, groups) * 2 + core})
    loads = [
        pltpu.make_async_copy(stripe_any, factor.at[me], load.at[0]),
        pltpu.make_async_copy(inverse_any.at[0], inverse, load.at[1]),
        pltpu.make_async_copy(sides_any, sides, load.at[2]),
        pltpu.make_async_copy(watts_any, watts_in, load.at[3]),
        pltpu.make_async_copy(structure_any, keeps, load.at[4]),
    ]
    for copy in loads:
        copy.start()

    loads[0].wait()
    pl.semaphore_wait(barrier, groups + supers + xs - 2)

    def factor_copy(b, send, where):
        return pltpu.make_async_remote_copy(
            src_ref=factor.at[b], dst_ref=factor.at[b], send_sem=send,
            recv_sem=factor_recv.at[b], device_id={"rhs": where},
        )

    def forward_copy(t, k, where):
        return pltpu.make_async_remote_copy(
            src_ref=fwd, dst_ref=fwd_in.at[t], send_sem=f_send.at[k],
            recv_sem=f_recv.at[t], device_id={"fac": where},
        )

    cuts = ((upd_out_a, upd_in_a, 0, 256), (upd_out_b, upd_in_b, 256, width))

    def update_copy(t, where, half):
        return pltpu.make_async_remote_copy(
            src_ref=cuts[half][0].at[where], dst_ref=cuts[half][1].at[t],
            send_sem=u_send.at[where, half], recv_sem=u_recv.at[t, half],
            device_id={"fac": where},
        )

    @pl.when(needed(me))
    def _():
        for zz in range(zs - 1, -1, -1):
            @pl.when(zz != z)
            def _():
                factor_copy(me, z_send.at[zz], rank(zz, x, core)).start()

    def relay(k):
        b = rank(lax.rem(z + zs - k, zs), x, core)

        @pl.when(needed(b))
        def _():
            if k > 0:
                factor_copy(b, z_send.at[0], me).wait_recv()
            for j in range(1, xs):
                other = lax.rem(x + j, xs)
                factor_copy(b, x_send.at[k, j], rank(z, other, core)).start()
                factor_copy(b, c_send.at[k, j], rank(z, other, 1 - core)).start()
            factor_copy(b, c_send.at[k, 0], rank(z, x, 1 - core)).start()

    relay(0)

    loads[1].wait()
    high, low = split(inverse[...])
    plain[:width] = high
    plain[width:] = low
    turned[:, :width] = high
    turned[:, width:] = low
    loads[2].wait()
    loads[4].wait()

    def twice(value):
        return jnp.concatenate([value, value], axis=1)

    @pl.when(s == 0)
    def _():
        fwd[...] = mul(twice(sides[...]), turned[...], NT).astype(BF16)
        for k in range(1, supers):
            forward_copy(0, k, k).start()

    for k in range(1, zs):
        relay(k)
    for k in range(zs):
        for j in range(1, xs):
            b = rank(lax.rem(z + zs - k, zs), lax.rem(x + xs - j, xs), core)

            @pl.when(needed(b))
            def _():
                factor_copy(b, z_send.at[0], me).wait_recv()

    loads[3].wait()
    watts[...] = watts_in[...].astype(F32).T.reshape(watts.shape)
    for g in range(groups):
        watts_own[g] = watts[2 * g + 1 - core]
        watts_own[groups + g] = watts[2 * g + core]

    for zz in range(zs):
        for xx in range(xs):
            b = rank(zz, xx, 1 - core)

            @pl.when(needed(b))
            def _():
                factor_copy(b, z_send.at[0], me).wait_recv()

    def block(t):
        return factor[t * per:(t + 1) * per].reshape(width, width)

    @pl.when(s > 0)
    def _():
        base[...] = sides[...].astype(F32)
        for t in range(supers - 1):
            @pl.when(s > t)
            def _():
                forward_copy(t, 0, s).wait_recv()
                keep = keeps[s, t].astype(F32)
                base[...] -= keep * mul(fwd_in[t], block(t), NN)
        fwd[...] = mul(twice(base[...].astype(BF16)), turned[...], NT).astype(BF16)
        for k in range(2, supers):
            @pl.when(s < k)
            def _():
                forward_copy(s, k, k).start()

    base[...] = mul(twice(fwd[...]), plain[...], NN)
    out_ref[...] = base[...].astype(BF16)
    for t in range(supers - 1, 0, -1):
        @pl.when(s < t)
        def _():
            for half, (_, arrived, first, end) in enumerate(cuts):
                update_copy(t, s, half).wait_recv()
                base[...] -= mul(arrived[t], plain[first:end], NN)
            if t - 1 == 0:
                out_ref[...] = base[...].astype(BF16)
            else:
                @pl.when(s == t - 1)
                def _():
                    out_ref[...] = base[...].astype(BF16)
    for t in range(supers - 2, -1, -1):
        @pl.when(s > t)
        def _():
            keep = keeps[s, t].astype(F32)
            for half, (leaving, _, first, end) in enumerate(cuts):
                rows = block(t)[first:end]
                leaving[t] = (keep * mul(out_ref[...], rows, NT)).astype(BF16)
                update_copy(s, t, half).start()

    def product(first):
        rows = watts_own[first:first + groups]
        rows = rows.reshape(groups * rows.shape[1], rows.shape[2]).astype(BF16)
        return mul(rows, out_ref[...], NN).reshape(mine.shape)

    pair_out[...] = product(0).astype(pair_out.dtype)
    pair = pltpu.make_async_remote_copy(
        src_ref=pair_out, dst_ref=pair_in, send_sem=pair_send, recv_sem=pair_recv,
        device_id={"rhs": rank(z, x, 1 - core)},
    )
    pair.start()
    mine[...] = product(groups)
    pair.wait_recv()
    both = mine[...] + pair_in[...].astype(F32)
    mine[...] = both
    sum_out[...] = both.astype(sum_out.dtype)

    def sum_copy(target, source, k):
        return pltpu.make_async_remote_copy(
            src_ref=sum_out.at[target], dst_ref=sum_in.at[source], send_sem=s_send.at[k],
            recv_sem=s_recv.at[source], device_id={"rhs": target * 2 + core},
        )

    step = jnp.where(2 * z >= zs, 1, groups - 1)
    for k in range(1, groups):
        sum_copy(lax.rem(chip + k * step, groups), chip, k).start()
    total = mine[chip]
    for k in range(1, groups):
        source = lax.rem(chip + groups - k, groups)
        sum_copy(chip, source, 0).wait_recv()
        total = total + sum_in[source].astype(F32)
    reply_ref[...] = total

    for k in range(1, groups):
        sum_copy(lax.rem(chip + k * step, groups), chip, k).wait_send()
    pair.wait_send()
    for t in range(supers - 1):
        @pl.when(s > t)
        def _():
            for half in range(2):
                update_copy(s, t, half).wait_send()
    for k in range(1, supers):
        @pl.when(s < k)
        def _():
            forward_copy(s, k, k).wait_send()

    @pl.when(needed(me))
    def _():
        for zz in range(zs):
            @pl.when(zz != z)
            def _():
                factor_copy(me, z_send.at[zz], me).wait_send()
    for k in range(zs):
        own = rank(lax.rem(z + zs - k, zs), x, core)

        @pl.when(needed(own))
        def _():
            factor_copy(own, c_send.at[k, 0], me).wait_send()
            for j in range(1, xs):
                factor_copy(own, x_send.at[k, j], me).wait_send()
                factor_copy(own, c_send.at[k, j], me).wait_send()


def write_out(solved_ref, reply_ref, solved_out, reply_out, sem):
    first = pltpu.make_async_copy(solved_ref, solved_out, sem.at[0])
    second = pltpu.make_async_copy(reply_ref, reply_out, sem.at[1])
    first.start()
    second.start()
    first.wait()
    second.wait()


def body(right_sides, stripe, inverses, structure, heater_wattages):
    supers = lax.axis_size("fac")
    ranks = lax.axis_size("rhs")
    zs = 4
    xs = ranks // (2 * zs)
    count, width = right_sides.shape
    columns = stripe.shape[1]
    loads = heater_wattages.shape[0]
    rows = loads // ranks
    groups = ranks // 2
    wire = BF16 if rows % 16 == 0 else F32
    dma = pltpu.SemaphoreType.DMA
    vmem = pl.BlockSpec(memory_space=pltpu.VMEM)
    whole = pl.BlockSpec(memory_space=pl.ANY)
    solved, reply = pl.pallas_call(
        functools.partial(kernel, (supers, ranks, zs, xs)),
        out_shape=(
            pltpu.VMEM((count, width), BF16),
            pltpu.VMEM((rows, width), F32),
        ),
        in_specs=[whole] * 5,
        out_specs=(vmem, vmem),
        scratch_shapes=[
            pltpu.VMEM((ranks, columns, width), BF16),
            pltpu.VMEM((count, width), BF16),
            pltpu.VMEM((width, width), F32),
            pltpu.SMEM((supers, supers), jnp.int32),
            pltpu.VMEM((count, loads), BF16),
            pltpu.VMEM((ranks, rows, count), F32),
            pltpu.VMEM((ranks, rows, count), F32),
            pltpu.VMEM((2 * width, width), BF16),
            pltpu.VMEM((width, 2 * width), BF16),
            pltpu.VMEM((count, width), F32),
            pltpu.VMEM((count, width), BF16),
            pltpu.VMEM((supers, count, width), BF16),
            pltpu.VMEM((supers, count, 256), BF16),
            pltpu.VMEM((supers, count, width - 256), BF16),
            pltpu.VMEM((supers, count, 256), BF16),
            pltpu.VMEM((supers, count, width - 256), BF16),
            pltpu.VMEM((groups, rows, width), wire),
            pltpu.VMEM((groups, rows, width), wire),
            pltpu.VMEM((groups, rows, width), F32),
            pltpu.VMEM((groups, rows, width), wire),
            pltpu.VMEM((groups, rows, width), wire),
            dma((5,)), dma((zs,)), dma((zs, xs)), dma((zs, xs)), dma((ranks,)),
            dma((supers,)), dma((supers,)), dma((supers, 2)), dma((supers, 2)),
            dma, dma, dma((groups,)), dma((groups,)),
        ],
        compiler_params=pltpu.CompilerParams(
            collective_id=0, has_side_effects=True, vmem_limit_bytes=LIMIT
        ),
    )(*(
        pltpu.with_memory_space_constraint(value, pltpu.HBM)
        for value in (right_sides, stripe.T, inverses, structure, heater_wattages.T)
    ))
    return pl.pallas_call(
        write_out,
        out_shape=(
            jax.ShapeDtypeStruct((count, width), BF16),
            jax.ShapeDtypeStruct((rows, width), F32),
        ),
        in_specs=[vmem, vmem],
        out_specs=(whole, whole),
        scratch_shapes=[dma((2,))],
    )(
        pltpu.with_memory_space_constraint(solved, pltpu.VMEM),
        pltpu.with_memory_space_constraint(reply, pltpu.VMEM),
    )


def solution(mesh):
    placed = (P("rhs", "fac"), P("fac", "rhs"), P("fac", None, None), P(), P(None, "rhs"))
    return jax.shard_map(
        body,
        mesh=mesh,
        in_specs=placed,
        out_specs=(P("rhs", "fac"), P("rhs", "fac")),
        check_vma=False,
    )
```

```python
import functools

import jax
import jax.numpy as jnp
from jax import lax
from jax.experimental import pallas as pl
from jax.experimental.pallas import tpu as pltpu
from jax.sharding import PartitionSpec as P

F32 = jnp.float32
BF16 = jnp.bfloat16
LIMIT = 32 * 1024 * 1024
NT = (((1,), (1,)), ((), ()))
NN = (((1,), (0,)), ((), ()))


def mul(left, right, dims):
    return lax.dot_general(left, right, dims, preferred_element_type=F32)


def split(value):
    high = value.astype(BF16)
    return high, (value - high.astype(F32)).astype(BF16)


def kernel(
    shape, sides_any, stripe_any, inverse_any, structure_any, watts_any, out_ref, reply_ref,
    factor, sides, inverse, keeps, watts_in, watts, watts_own, plain, turned, base, fwd, fwd_in,
    upd_out_a, upd_out_b, upd_in_a, upd_in_b, pair_out, pair_in, mine, sum_out, sum_in,
    load, z_send, x_send, c_send, factor_recv, f_send, f_recv, u_send, u_recv,
    pair_send, pair_recv, s_send, s_recv,
):
    supers, ranks, zs, xs = shape
    groups = ranks // 2
    width = inverse.shape[0]
    per = width // factor.shape[1]
    s = lax.axis_index("fac")
    me = lax.axis_index("rhs")
    core = lax.rem(me, 2)
    chip = lax.div(me, 2)
    x = lax.rem(chip, xs)
    z = lax.div(chip, xs)

    def rank(zz, xx, cc):
        return (zz * xs + xx) * 2 + cc

    def needed(b):
        return b < s * per

    barrier = pltpu.get_barrier_semaphore()
    pl.semaphore_signal(barrier, inc=1, device_id={"rhs": chip * 2 + 1 - core})
    for j in range(1, xs):
        beside = rank(z, lax.rem(x + j, xs), 1 - core)
        pl.semaphore_signal(barrier, inc=1, device_id={"rhs": beside})
    for k in range(1, supers):
        pl.semaphore_signal(barrier, inc=1, device_id={"fac": lax.rem(s + k, supers)})
    for k in range(1, groups):
        pl.semaphore_signal(barrier, inc=1, device_id={"rhs": lax.rem(chip + k, groups) * 2 + core})
    loads = [
        pltpu.make_async_copy(stripe_any, factor.at[me], load.at[0]),
        pltpu.make_async_copy(inverse_any.at[0], inverse, load.at[1]),
        pltpu.make_async_copy(sides_any, sides, load.at[2]),
        pltpu.make_async_copy(watts_any, watts_in, load.at[3]),
        pltpu.make_async_copy(structure_any, keeps, load.at[4]),
    ]
    for copy in loads:
        copy.start()

    loads[0].wait()
    pl.semaphore_wait(barrier, groups + supers + xs - 2)

    def factor_copy(b, send, where):
        return pltpu.make_async_remote_copy(
            src_ref=factor.at[b], dst_ref=factor.at[b], send_sem=send,
            recv_sem=factor_recv.at[b], device_id={"rhs": where},
        )

    def forward_copy(t, k, where):
        return pltpu.make_async_remote_copy(
            src_ref=fwd, dst_ref=fwd_in.at[t], send_sem=f_send.at[k],
            recv_sem=f_recv.at[t], device_id={"fac": where},
        )

    cuts = ((upd_out_a, upd_in_a, 0, 256), (upd_out_b, upd_in_b, 256, width))

    def update_copy(t, where, half):
        return pltpu.make_async_remote_copy(
            src_ref=cuts[half][0].at[where], dst_ref=cuts[half][1].at[t],
            send_sem=u_send.at[where, half], recv_sem=u_recv.at[t, half],
            device_id={"fac": where},
        )

    @pl.when(needed(me))
    def _():
        for zz in range(zs - 1, -1, -1):
            @pl.when(zz != z)
            def _():
                factor_copy(me, z_send.at[zz], rank(zz, x, core)).start()

    def relay(k):
        b = rank(lax.rem(z + zs - k, zs), x, core)

        @pl.when(needed(b))
        def _():
            if k > 0:
                factor_copy(b, z_send.at[0], me).wait_recv()
            for j in range(1, xs):
                other = lax.rem(x + j, xs)
                factor_copy(b, x_send.at[k, j], rank(z, other, core)).start()
                factor_copy(b, c_send.at[k, j], rank(z, other, 1 - core)).start()
            factor_copy(b, c_send.at[k, 0], rank(z, x, 1 - core)).start()

    for k in range(zs):
        relay(k)

    loads[1].wait()
    high, low = split(inverse[...])
    plain[:width] = high
    plain[width:] = low
    turned[:, :width] = high
    turned[:, width:] = low
    loads[2].wait()
    loads[4].wait()

    def twice(value):
        return jnp.concatenate([value, value], axis=1)

    @pl.when(s == 0)
    def _():
        fwd[...] = mul(twice(sides[...]), turned[...], NT).astype(BF16)
        for k in range(1, supers):
            forward_copy(0, k, k).start()

    for k in range(zs):
        for j in range(1, xs):
            b = rank(lax.rem(z + zs - k, zs), lax.rem(x + xs - j, xs), core)

            @pl.when(needed(b))
            def _():
                factor_copy(b, z_send.at[0], me).wait_recv()

    loads[3].wait()
    watts[...] = watts_in[...].astype(F32).T.reshape(watts.shape)
    for g in range(groups):
        watts_own[g] = watts[2 * g + 1 - core]
        watts_own[groups + g] = watts[2 * g + core]

    for zz in range(zs):
        for xx in range(xs):
            b = rank(zz, xx, 1 - core)

            @pl.when(needed(b))
            def _():
                factor_copy(b, z_send.at[0], me).wait_recv()

    def block(t):
        return factor[t * per:(t + 1) * per].reshape(width, width)

    @pl.when(s > 0)
    def _():
        base[...] = sides[...].astype(F32)
        for t in range(supers - 1):
            @pl.when(s > t)
            def _():
                forward_copy(t, 0, s).wait_recv()
                keep = keeps[s, t].astype(F32)
                base[...] -= keep * mul(fwd_in[t], block(t), NN)
        fwd[...] = mul(twice(base[...].astype(BF16)), turned[...], NT).astype(BF16)
        for k in range(2, supers):
            @pl.when(s < k)
            def _():
                forward_copy(s, k, k).start()

    base[...] = mul(twice(fwd[...]), plain[...], NN)
    out_ref[...] = base[...].astype(BF16)
    for t in range(supers - 1, 0, -1):
        @pl.when(s < t)
        def _():
            for half, (_, arrived, first, end) in enumerate(cuts):
                update_copy(t, s, half).wait_recv()
                base[...] -= mul(arrived[t], plain[first:end], NN)
            if t - 1 == 0:
                out_ref[...] = base[...].astype(BF16)
            else:
                @pl.when(s == t - 1)
                def _():
                    out_ref[...] = base[...].astype(BF16)
    for t in range(supers - 2, -1, -1):
        @pl.when(s > t)
        def _():
            keep = keeps[s, t].astype(F32)
            for half, (leaving, _, first, end) in enumerate(cuts):
                rows = block(t)[first:end]
                leaving[t] = (keep * mul(out_ref[...], rows, NT)).astype(BF16)
                update_copy(s, t, half).start()

    def product(first):
        rows = watts_own[first:first + groups]
        rows = rows.reshape(groups * rows.shape[1], rows.shape[2]).astype(BF16)
        return mul(rows, out_ref[...], NN).reshape(mine.shape)

    pair_out[...] = product(0).astype(pair_out.dtype)
    pair = pltpu.make_async_remote_copy(
        src_ref=pair_out, dst_ref=pair_in, send_sem=pair_send, recv_sem=pair_recv,
        device_id={"rhs": rank(z, x, 1 - core)},
    )
    pair.start()
    mine[...] = product(groups)
    pair.wait_recv()
    both = mine[...] + pair_in[...].astype(F32)
    mine[...] = both
    sum_out[...] = both.astype(sum_out.dtype)

    def sum_copy(target, source, k):
        return pltpu.make_async_remote_copy(
            src_ref=sum_out.at[target], dst_ref=sum_in.at[source], send_sem=s_send.at[k],
            recv_sem=s_recv.at[source], device_id={"rhs": target * 2 + core},
        )

    step = jnp.where(2 * z >= zs, 1, groups - 1)
    for k in range(1, groups):
        sum_copy(lax.rem(chip + k * step, groups), chip, k).start()
    total = mine[chip]
    for k in range(1, groups):
        source = lax.rem(chip + groups - k, groups)
        sum_copy(chip, source, 0).wait_recv()
        total = total + sum_in[source].astype(F32)
    reply_ref[...] = total

    for k in range(1, groups):
        sum_copy(lax.rem(chip + k * step, groups), chip, k).wait_send()
    pair.wait_send()
    for t in range(supers - 1):
        @pl.when(s > t)
        def _():
            for half in range(2):
                update_copy(s, t, half).wait_send()
    for k in range(1, supers):
        @pl.when(s < k)
        def _():
            forward_copy(s, k, k).wait_send()

    @pl.when(needed(me))
    def _():
        for zz in range(zs):
            @pl.when(zz != z)
            def _():
                factor_copy(me, z_send.at[zz], me).wait_send()
    for k in range(zs):
        own = rank(lax.rem(z + zs - k, zs), x, core)

        @pl.when(needed(own))
        def _():
            factor_copy(own, c_send.at[k, 0], me).wait_send()
            for j in range(1, xs):
                factor_copy(own, x_send.at[k, j], me).wait_send()
                factor_copy(own, c_send.at[k, j], me).wait_send()


def write_out(solved_ref, reply_ref, solved_out, reply_out, sem):
    first = pltpu.make_async_copy(solved_ref, solved_out, sem.at[0])
    second = pltpu.make_async_copy(reply_ref, reply_out, sem.at[1])
    first.start()
    second.start()
    first.wait()
    second.wait()


def body(right_sides, stripe, inverses, structure, heater_wattages):
    supers = lax.axis_size("fac")
    ranks = lax.axis_size("rhs")
    zs = 4
    xs = ranks // (2 * zs)
    count, width = right_sides.shape
    columns = stripe.shape[1]
    loads = heater_wattages.shape[0]
    rows = loads // ranks
    groups = ranks // 2
    wire = BF16 if rows % 16 == 0 else F32
    dma = pltpu.SemaphoreType.DMA
    vmem = pl.BlockSpec(memory_space=pltpu.VMEM)
    whole = pl.BlockSpec(memory_space=pl.ANY)
    solved, reply = pl.pallas_call(
        functools.partial(kernel, (supers, ranks, zs, xs)),
        out_shape=(
            pltpu.VMEM((count, width), BF16),
            pltpu.VMEM((rows, width), F32),
        ),
        in_specs=[whole] * 5,
        out_specs=(vmem, vmem),
        scratch_shapes=[
            pltpu.VMEM((ranks, columns, width), BF16),
            pltpu.VMEM((count, width), BF16),
            pltpu.VMEM((width, width), F32),
            pltpu.SMEM((supers, supers), jnp.int32),
            pltpu.VMEM((count, loads), BF16),
            pltpu.VMEM((ranks, rows, count), F32),
            pltpu.VMEM((ranks, rows, count), F32),
            pltpu.VMEM((2 * width, width), BF16),
            pltpu.VMEM((width, 2 * width), BF16),
            pltpu.VMEM((count, width), F32),
            pltpu.VMEM((count, width), BF16),
            pltpu.VMEM((supers, count, width), BF16),
            pltpu.VMEM((supers, count, 256), BF16),
            pltpu.VMEM((supers, count, width - 256), BF16),
            pltpu.VMEM((supers, count, 256), BF16),
            pltpu.VMEM((supers, count, width - 256), BF16),
            pltpu.VMEM((groups, rows, width), wire),
            pltpu.VMEM((groups, rows, width), wire),
            pltpu.VMEM((groups, rows, width), F32),
            pltpu.VMEM((groups, rows, width), wire),
            pltpu.VMEM((groups, rows, width), wire),
            dma((5,)), dma((zs,)), dma((zs, xs)), dma((zs, xs)), dma((ranks,)),
            dma((supers,)), dma((supers,)), dma((supers, 2)), dma((supers, 2)),
            dma, dma, dma((groups,)), dma((groups,)),
        ],
        compiler_params=pltpu.CompilerParams(
            collective_id=0, has_side_effects=True, vmem_limit_bytes=LIMIT
        ),
    )(*(
        pltpu.with_memory_space_constraint(value, pltpu.HBM)
        for value in (right_sides, stripe.T, inverses, structure, heater_wattages.T)
    ))
    return pl.pallas_call(
        write_out,
        out_shape=(
            jax.ShapeDtypeStruct((count, width), BF16),
            jax.ShapeDtypeStruct((rows, width), F32),
        ),
        in_specs=[vmem, vmem],
        out_specs=(whole, whole),
        scratch_shapes=[dma((2,))],
    )(
        pltpu.with_memory_space_constraint(solved, pltpu.VMEM),
        pltpu.with_memory_space_constraint(reply, pltpu.VMEM),
    )


def solution(mesh):
    placed = (P("rhs", "fac"), P("fac", "rhs"), P("fac", None, None), P(), P(None, "rhs"))
    return jax.shard_map(
        body,
        mesh=mesh,
        in_specs=placed,
        out_specs=(P("rhs", "fac"), P("rhs", "fac")),
        check_vma=False,
    )
```
